128 devices in a mesh: op: 8 (over x, core), sec: 16 (over z, y).
Axes of the slice: x: 4, y: 4, z: 4, core: 2. Of those that a mesh axis runs over, the one named last changes fastest.
Arguments:
- start_vector: float32 [16, 256, 256], P('sec'), may hold values from -6 to 6
- diag_guess: float32 [16, 256, 256], P('sec'), may hold values from -4 to 4
- left_env: bfloat16 [8192, 256, 256], P(('op', 'sec')), may hold values from -0.015625 to 0.015625
- right_env: bfloat16 [8192, 256, 256], P(('op', 'sec')), may hold values from -0.375 to 0.375
- sector_from: int32 [8192], P(('op', 'sec')), may hold values from 0 to 15
- sector_to: int32 [8192], P(('op', 'sec')), may hold values from 0 to 15
- term_count: int32 [128], P(('op', 'sec')), may hold values from 1 to 64, as said below
Outputs:
- ritz_vector: float32 [16, 256, 256], P('sec')
- ritz_residual: float32 [16, 256, 256], P('sec')
The draws below stay inside these ranges and needn't reach their ends.
Inputs may be any that keep to these rules, and one draw needn't show every extreme that they name: `term_count`: every device holds at least one live term, and some device has all 64 slots live.
All inputs are finite; a program needn't handle non-finite values.
Results may differ from the reference program's by a relative error of at most 0.0044.
The reference program's roundings to bfloat16 on the way count: a program that leaves them out, or rounds other values in their place, can miss the bound.
Values may be sent and summed in bfloat16 or wider, within the bound.
No kernel may reach another device: no remote copies, remote signals or barrier semaphores. Data moves between devices by JAX's collectives and lax.ppermute only.
A program may use at most 128 MiB of HBM per device.

```python
import jax
import jax.numpy as jnp
from jax import lax

B = 256
S_DEV = 1
K_DEV = 64
SECTORS = 16
DEVS = 128
TERMS = 8192
N_OP = 8


def draw_term_count(key, part):
    key = jax.random.fold_in(key, 7)
    key_level = jax.random.fold_in(key, 1)
    key_spot = jax.random.fold_in(key, 2)
    levels = jax.random.randint(key_level, (DEVS,), 0, 3)
    counts = jnp.maximum(jnp.right_shift(jnp.int32(K_DEV), levels), 1)
    spot = jax.random.randint(key_spot, (), 0, DEVS)
    return counts.at[spot].set(K_DEV).astype(jnp.int32)


def touch_ends(values, key, low, largest):
    spot = [jax.random.randint(jax.random.fold_in(key, axis), (), 0, length) for axis, length in enumerate(values.shape)]
    widest = values.shape.index(max(values.shape))
    neighbour = spot[:widest] + [(spot[widest] + 1) % values.shape[widest]] + spot[widest + 1:]
    return values.at[tuple(spot)].set(low).at[tuple(neighbour)].set(largest)


def block_scale(stream_key, shape, split, smallest, top_value):
    def one(axis_at, shards_of):
        draws = jax.random.uniform(jax.random.fold_in(jax.random.fold_in(stream_key, 6), axis_at), (shards_of,), jnp.float32, smallest / len(split), top_value / len(split))
        return jnp.repeat(jnp.exp(draws), shape[axis_at] // shards_of).reshape((-1,) + (1,) * (len(shape) - axis_at - 1))

    factor_of = one(*split[0])
    for cut in split[1:]:
        factor_of = factor_of * one(*cut)
    return factor_of


def scatter_about(stream_key, extent, deviation, reach, cuts=(), kind=jnp.bfloat16):
    array = jax.random.normal(stream_key, extent, jnp.float32) * deviation
    if len(cuts) > 0:
        array = block_scale(stream_key, extent, cuts, -0.22, 0.18) * array
    return jnp.clip(array, min=-reach, max=reach).astype(kind)


def setup_inputs(seed: int = 0) -> dict:
    seeds = jax.random.split(jax.random.key(seed), 8)
    start_vector = scatter_about(seeds[0], (SECTORS, B, B), 1.0, 6.0, ((0, 16),), jnp.float32)
    diag_guess = jnp.clip(jax.random.uniform(seeds[1], (SECTORS, B, B), jnp.float32, -4.0, 4.0) * block_scale(seeds[1], (SECTORS, B, B), ((0, 16),), -0.4, 0.0), -4.0, 4.0)
    left_env = scatter_about(seeds[2], (TERMS, B, B), (B * K_DEV * N_OP // S_DEV) ** -0.5, 0.015625, ((0, 128),))
    right_env = scatter_about(seeds[3], (TERMS, B, B), B ** -0.5, 0.375, ((0, 128),))
    sector_from = touch_ends(jax.random.randint(seeds[4], (TERMS,), 0, SECTORS), jax.random.fold_in(seeds[4], 1), 0, SECTORS - 1).astype(jnp.int32)
    sector_to = touch_ends(jax.random.randint(seeds[5], (TERMS,), 0, SECTORS), jax.random.fold_in(seeds[5], 1), 0, SECTORS - 1).astype(jnp.int32)
    term_count = draw_term_count(jax.random.fold_in(seeds[7], 71), 0)
    return dict(start_vector=start_vector, diag_guess=diag_guess, left_env=left_env, right_env=right_env, sector_from=sector_from, sector_to=sector_to, term_count=term_count)


def apply_ham(vector, left_env, right_env, sector_from, sector_to, term_count):
    blocks = vector.astype(jnp.bfloat16)
    slots = jnp.arange(left_env.shape[0], dtype=jnp.int32)
    live_mask = (slots % K_DEV < term_count[slots // K_DEV]).astype(jnp.float32)

    def add_term(accum, item):
        left_block, right_block, source, target, alive = item
        first = jnp.dot(left_block, blocks[source], preferred_element_type=jnp.float32).astype(jnp.bfloat16)
        forward = jnp.dot(first, right_block.T, preferred_element_type=jnp.float32)
        second = jnp.dot(left_block.T, blocks[target], preferred_element_type=jnp.float32).astype(jnp.bfloat16)
        backward = jnp.dot(second, right_block, preferred_element_type=jnp.float32)
        accum = accum.at[target].add(alive * forward)
        accum = accum.at[source].add(alive * backward)
        return (accum, None)
    start = jnp.zeros(vector.shape, jnp.float32)
    result, unused = lax.scan(add_term, start, (left_env, right_env, sector_from, sector_to, live_mask))
    return result

def reference(start_vector, diag_guess, left_env, right_env, sector_from, sector_to, term_count):

    def inner(first_arr, second_arr):
        return jnp.mean(first_arr * second_arr)
    vec_one = start_vector / jnp.sqrt(inner(start_vector, start_vector) + 1e-06)
    sigma_one = apply_ham(vec_one, left_env, right_env, sector_from, sector_to, term_count)
    theta = inner(vec_one, sigma_one)
    resid_one = sigma_one - theta * vec_one
    correction = resid_one / jnp.maximum(jnp.abs(diag_guess - theta), 1.0)
    ortho = correction - inner(vec_one, correction) * vec_one
    vec_two = ortho / jnp.sqrt(inner(ortho, ortho) + 1e-06)
    sigma_two = apply_ham(vec_two, left_env, right_env, sector_from, sector_to, term_count)
    beta = inner(vec_one, sigma_two)
    gamma = inner(vec_two, sigma_two)
    lowest = 0.5 * (theta + gamma) - jnp.sqrt((0.5 * (theta - gamma)) ** 2 + beta * beta)
    norm_scale = jnp.sqrt(beta * beta + (lowest - theta) ** 2)
    coef_one = beta / norm_scale
    coef_two = (lowest - theta) / norm_scale
    ritz_vector = coef_one * vec_one + coef_two * vec_two
    ritz_residual = coef_one * sigma_one + coef_two * sigma_two - lowest * ritz_vector
    return (ritz_vector, ritz_residual)
```

```python
import jax
import jax.numpy as jnp
from jax import lax
from jax.experimental import pallas as pl
from jax.experimental.pallas import tpu as pltpu
from jax.sharding import PartitionSpec as P

F32, BF16 = jnp.float32, jnp.bfloat16
SEC, B, ROWS, LANES = 16, 256, 32, 128
CHIPS_X, N_OP = 4, 8
PIECES = CHIPS_X * SEC
TERMS, STEP = 64, 8
ENTRIES = SEC * B * B
CORE_SWAP = [(i, i ^ 1) for i in range(N_OP)]
GROUPS = [[(2 * x + core) * SEC + s for x in range(CHIPS_X) for s in range(SEC)] for core in range(2)]
VMEM = pltpu.CompilerParams(vmem_limit_bytes=56 << 20)


def dot(a, b, contract):
    return lax.dot_general(a, b, ((contract[:1], contract[1:]), ((), ())), preferred_element_type=F32)


def fold(block):
    return jnp.sum(block.reshape(-1, 8, LANES), axis=0)


def block_rows(x, core):
    return pl.ds(pl.multiple_of((2 * x + core) * ROWS, ROWS), ROWS)


def apply_terms(i, count_ref, from_ref, to_ref, x_ref, left_ref, right_ref, acc_ref):
    live = count_ref[0] - i * STEP

    def halves(j):
        source, target = from_ref[i * STEP + j], to_ref[i * STEP + j]
        first = dot(left_ref[j], x_ref[source], (1, 0)).astype(BF16)
        second = dot(left_ref[j], x_ref[target], (0, 0)).astype(BF16)
        return j, source, target, first, second

    def add(j, source, target, first, second):
        acc_ref[target] += dot(first, right_ref[j], (1, 1))
        acc_ref[source] += dot(second, right_ref[j], (1, 0))

    @pl.when(live >= STEP)
    def _():
        held = halves(0)
        for j in range(1, STEP):
            ahead = halves(j)
            add(*held)
            held = ahead
        add(*held)

    @pl.when((live > 0) & (live < STEP))
    def _():
        @pl.loop(0, live)
        def _(j):
            add(*halves(j))


def split_out(core, acc_ref, keep_ref, send_ref):
    @pl.loop(0, SEC)
    def _(s):
        for x in range(CHIPS_X):
            mine = acc_ref[s, block_rows(x, core), :]
            theirs = acc_ref[s, block_rows(x, 1 - core), :].astype(BF16)
            keep_ref[x * SEC + s, :ROWS, :] = mine[:, :LANES]
            keep_ref[x * SEC + s, ROWS:, :] = mine[:, LANES:]
            send_ref[x * SEC + s, :ROWS, :] = theirs[:, :LANES]
            send_ref[x * SEC + s, ROWS:, :] = theirs[:, LANES:]


def first_kernel(count_ref, from_ref, to_ref, at_ref, own_ref, other_ref, left_ref, right_ref,
                 v_ref, piece_ref, keep_ref, send_ref, sums_ref, x_ref, acc_ref):
    i = pl.program_id(0)
    core, sector = at_ref[0], at_ref[1]

    @pl.when(i == 0)
    def _():
        def squares(s, total):
            return total + fold(own_ref[s] * own_ref[s]) + fold(other_ref[s] * other_ref[s])

        total = lax.fori_loop(0, SEC, squares, jnp.zeros((8, LANES), F32))
        scale = 1.0 / jnp.sqrt(jnp.sum(total, keepdims=True) / ENTRIES + 1e-06)

        @pl.loop(0, SEC)
        def _(s):
            for x in range(CHIPS_X):
                for ref, at in ((own_ref, core), (other_ref, 1 - core)):
                    block = ref[s, x * ROWS:(x + 1) * ROWS, :] * scale
                    v_ref[s, block_rows(x, at), :] = block
                    x_ref[s, block_rows(x, at), :] = block.astype(BF16)
            acc_ref[s] = jnp.zeros((B, B), F32)

    apply_terms(i, count_ref, from_ref, to_ref, x_ref, left_ref, right_ref, acc_ref)

    @pl.when(i == pl.num_programs(0) - 1)
    def _():
        split_out(core, acc_ref, keep_ref, send_ref)

        def inner(s, total):
            return total + fold(v_ref[s] * acc_ref[s])

        theta = lax.fori_loop(0, SEC, inner, jnp.zeros((8, LANES), F32))
        sums_ref[0] = theta
        sums_ref[1] = jnp.zeros_like(theta)
        block = v_ref[sector, block_rows(at_ref[2], core), :]
        piece_ref[:ROWS, :] = block[:, :LANES]
        piece_ref[ROWS:, :] = block[:, LANES:]


def second_kernel(count_ref, from_ref, to_ref, at_ref, own_ref, other_ref, v_ref, left_ref, right_ref,
                  v2s_ref, keep_ref, send_ref, sums_ref, v2_ref, x_ref, acc_ref):
    i = pl.program_id(0)
    core, sector = at_ref[0], at_ref[1]
    zero = jnp.zeros((8, LANES), F32)

    def blocks(s):
        for x in range(CHIPS_X):
            for ref, at in ((own_ref, core), (other_ref, 1 - core)):
                for h in range(2):
                    corr = ref[x * SEC + s, h * ROWS:(h + 1) * ROWS, :]
                    yield corr, (s, block_rows(x, at), slice(h * LANES, (h + 1) * LANES))

    @pl.when(i == 0)
    def _():
        def project(s, total):
            for corr, at in blocks(s):
                total = total + fold(v_ref[at] * corr)
            return total

        along = jnp.sum(lax.fori_loop(0, SEC, project, zero), keepdims=True) / ENTRIES

        def remove(s, total):
            for corr, at in blocks(s):
                ortho = corr - along * v_ref[at]
                v2_ref[at] = ortho
                total = total + fold(ortho * ortho)
            acc_ref[s] = jnp.zeros((B, B), F32)
            return total

        ortho_sq = jnp.sum(lax.fori_loop(0, SEC, remove, zero), keepdims=True) / ENTRIES
        scale = 1.0 / jnp.sqrt(ortho_sq + 1e-06)

        @pl.loop(0, SEC)
        def _(s):
            block = v2_ref[s] * scale
            v2_ref[s] = block
            x_ref[s] = block.astype(BF16)

        v2s_ref[...] = v2_ref[sector]

    apply_terms(i, count_ref, from_ref, to_ref, x_ref, left_ref, right_ref, acc_ref)

    @pl.when(i == pl.num_programs(0) - 1)
    def _():
        split_out(core, acc_ref, keep_ref, send_ref)

        def inner(s, totals):
            return totals[0] + fold(v_ref[s] * acc_ref[s]), totals[1] + fold(v2_ref[s] * acc_ref[s])

        sums_ref[0], sums_ref[1] = lax.fori_loop(0, SEC, inner, (zero, zero))


def join_kernel(keep_ref, got_ref, sums_ref, got_sums_ref, out_ref):
    row = lax.broadcasted_iota(jnp.int32, (16, LANES), 0)
    tile = jnp.zeros((16, LANES), F32)
    for k in range(2):
        rest = jnp.sum(sums_ref[k] + got_sums_ref[k], keepdims=True)
        for part in range(3):
            top = rest.astype(BF16).astype(F32)
            tile = jnp.where(row == 3 * k + part, top, tile)
            rest = rest - top
    tile = tile.astype(BF16)

    @pl.loop(0, PIECES)
    def _(p):
        out_ref[p, :2 * ROWS, :] = (keep_ref[p] + got_ref[p].astype(F32)).astype(BF16)
        out_ref[p, 2 * ROWS:, :] = tile


def gathered_sum(got_ref):
    def add(p, total):
        return total + got_ref[p].astype(F32)

    total = lax.fori_loop(0, PIECES, add, jnp.zeros((2 * ROWS + 16, LANES), F32))
    row = lax.broadcasted_iota(jnp.int32, (16, LANES), 0)
    tile = total[2 * ROWS:, :]
    scalars = [
        jnp.sum(jnp.where((row >= 3 * k) & (row < 3 * k + 3), tile, 0.0), keepdims=True) / (LANES * ENTRIES)
        for k in range(2)
    ]
    return total[:2 * ROWS, :], scalars


def correct_kernel(got_ref, v_ref, diag_ref, corr_ref, w_ref, theta_ref):
    sigma, (theta, _) = gathered_sum(got_ref)
    w_ref[...] = sigma
    theta_ref[...] = jnp.broadcast_to(theta, theta_ref.shape)
    corr = (sigma - theta * v_ref[...]) / jnp.maximum(jnp.abs(diag_ref[...] - theta), 1.0)

    @pl.loop(0, PIECES)
    def _(p):
        corr_ref[p] = corr


def ritz_kernel(at_ref, got_ref, v_ref, v2s_ref, w_ref, theta_ref, out_ref, coef_ref):
    sigma, (beta, gamma) = gathered_sum(got_ref)
    theta = theta_ref[:1, :1]
    lowest = 0.5 * (theta + gamma) - jnp.sqrt((0.5 * (theta - gamma)) ** 2 + beta * beta)
    norm = jnp.sqrt(beta * beta + (lowest - theta) ** 2)
    one, two = beta / norm, (lowest - theta) / norm
    coef_ref[0] = jnp.broadcast_to(one, (8, LANES))
    coef_ref[1] = jnp.broadcast_to(two, (8, LANES))
    v2 = v2s_ref[block_rows(at_ref[2], at_ref[0]), :]
    for h in range(2):
        rows, lanes = slice(h * ROWS, (h + 1) * ROWS), slice(h * LANES, (h + 1) * LANES)
        ritz = one * v_ref[rows, :] + two * v2[:, lanes]
        resid = one * w_ref[rows, :] + two * sigma[rows, :] - lowest * ritz
        for p in range(N_OP):
            out_ref[p, :, lanes] = resid


def shape(*dims, dtype=F32):
    return jax.ShapeDtypeStruct(dims, dtype)


SMEM = pl.BlockSpec(memory_space=pltpu.SMEM)
WHOLE = pl.BlockSpec(memory_space=pltpu.VMEM)
TERM_BLOCK = pl.BlockSpec((STEP, B, B), lambda i: (i, 0, 0))


def swap(x):
    return lax.ppermute(x, "op", CORE_SWAP)


def exchange(x):
    return lax.all_to_all(x, ("op", "sec"), 0, 0, tiled=True, axis_index_groups=GROUPS)


def two_lanes(rows):
    return jnp.concatenate([rows[:, :LANES], rows[:, LANES:]], axis=0)


def reduce_partial(keep, send, sums):
    payload = pl.pallas_call(
        join_kernel,
        out_shape=shape(PIECES, 2 * ROWS + 16, LANES, dtype=BF16),
        in_specs=[WHOLE] * 4,
        out_specs=WHOLE,
        compiler_params=VMEM,
        name="join",
    )(keep, swap(send), sums, swap(sums))
    return exchange(payload)


def per_device(start_vector, diag_guess, left_env, right_env, sector_from, sector_to, term_count):
    op, sector = lax.axis_index("op"), lax.axis_index("sec")
    core, chip = op % 2, op // 2
    at = jnp.stack([core, sector, chip]).astype(jnp.int32)
    terms = (term_count, sector_from, sector_to, at)

    mine = lax.dynamic_index_in_dim(start_vector.reshape(CHIPS_X, 2, ROWS, B), core, 1, keepdims=False)
    mine = jnp.broadcast_to(mine.reshape(1, B // 2, B), (SEC, B // 2, B))
    own = lax.all_to_all(mine, "sec", 0, 0, tiled=True)
    other = swap(own)
    diag = two_lanes(lax.dynamic_slice_in_dim(diag_guess[0], op * ROWS, ROWS, 0))

    split_shapes = [shape(PIECES, 2 * ROWS, LANES), shape(PIECES, 2 * ROWS, LANES, dtype=BF16), shape(2, 8, LANES)]
    vec, piece, keep, send, sums = pl.pallas_call(
        first_kernel,
        grid=(TERMS // STEP,),
        out_shape=[shape(SEC, B, B), shape(2 * ROWS, LANES)] + split_shapes,
        in_specs=[SMEM] * 4 + [WHOLE] * 2 + [TERM_BLOCK] * 2,
        out_specs=[WHOLE] * 5,
        scratch_shapes=[pltpu.VMEM((SEC, B, B), BF16), pltpu.VMEM((SEC, B, B), F32)],
        compiler_params=VMEM,
        name="first_apply",
    )(*terms, own, other, left_env, right_env)

    got = reduce_partial(keep, send, sums)
    corr, sigma_one, theta = pl.pallas_call(
        correct_kernel,
        out_shape=[shape(PIECES, 2 * ROWS, LANES), shape(2 * ROWS, LANES), shape(8, LANES)],
        in_specs=[WHOLE] * 3,
        out_specs=[WHOLE] * 3,
        compiler_params=VMEM,
        name="correct",
    )(got, piece, diag)

    own = exchange(corr)
    other = swap(own)
    vec_two, keep, send, sums = pl.pallas_call(
        second_kernel,
        grid=(TERMS // STEP,),
        out_shape=[shape(B, B)] + split_shapes,
        in_specs=[SMEM] * 4 + [WHOLE] * 3 + [TERM_BLOCK] * 2,
        out_specs=[WHOLE] * 4,
        scratch_shapes=[
            pltpu.VMEM((SEC, B, B), F32),
            pltpu.VMEM((SEC, B, B), BF16),
            pltpu.VMEM((SEC, B, B), F32),
        ],
        compiler_params=VMEM,
        name="second_apply",
    )(*terms, own, other, vec, left_env, right_env)

    got = reduce_partial(keep, send, sums)
    resid, coefs = pl.pallas_call(
        ritz_kernel,
        out_shape=[shape(N_OP, ROWS, B), shape(2, 8, LANES)],
        in_specs=[SMEM] + [WHOLE] * 5,
        out_specs=[WHOLE] * 2,
        compiler_params=VMEM,
        name="ritz",
    )(at, got, piece, vec_two, sigma_one, theta)

    ritz_residual = lax.all_to_all(resid, "op", 0, 0, tiled=True).reshape(1, B, B)
    vec_one = lax.dynamic_index_in_dim(vec, sector, 0, keepdims=True)
    ritz_vector = coefs[0, 0, 0] * vec_one + coefs[1, 0, 0] * vec_two[None]
    return (ritz_vector, ritz_residual)


def solution(mesh):
    return jax.shard_map(
        per_device,
        mesh=mesh,
        in_specs=(
            P("sec", None, None),
            P("sec", None, None),
            P(("op", "sec"), None, None),
            P(("op", "sec"), None, None),
            P(("op", "sec")),
            P(("op", "sec")),
            P(("op", "sec")),
        ),
        out_specs=(P("sec", None, None), P("sec", None, None)),
        check_vma=False,
    )
```

```python
import jax
import jax.numpy as jnp
from jax import lax
from jax.experimental import pallas as pl
from jax.experimental.pallas import tpu as pltpu
from jax.sharding import PartitionSpec as P

F32, BF16 = jnp.float32, jnp.bfloat16
SEC, B, ROWS, LANES = 16, 256, 32, 128
CHIPS_X, N_OP = 4, 8
PIECES = CHIPS_X * SEC
TERMS, GROUP, STEP = 64, 8, 16
ENTRIES = SEC * B * B
CORE_SWAP = [(i, i ^ 1) for i in range(N_OP)]
GROUPS = [[(2 * x + core) * SEC + s for x in range(CHIPS_X) for s in range(SEC)] for core in range(2)]


def dot(a, b, contract):
    return lax.dot_general(a, b, ((contract[:1], contract[1:]), ((), ())), preferred_element_type=F32)


def fold(block):
    block = block.reshape(-1, 8, block.shape[-1])
    block = jnp.sum(block, axis=0)
    return sum(block[:, k:k + LANES] for k in range(0, block.shape[-1], LANES))


def block_rows(x, core):
    return pl.ds(pl.multiple_of((2 * x + core) * ROWS, ROWS), ROWS)


def term_copies(i, left_ref, right_ref, left, right, sems):
    at = pl.ds(i * GROUP, GROUP)
    return (
        pltpu.make_async_copy(left_ref.at[at], left.at[at], sems.at[0, i]),
        pltpu.make_async_copy(right_ref.at[at], right.at[at], sems.at[1, i]),
    )


def start_terms(count_ref, *refs):
    for i in range(TERMS // GROUP):
        @pl.when(i * GROUP < count_ref[0])
        def _():
            for copy in term_copies(i, *refs):
                copy.start()


def apply_terms(count_ref, from_ref, to_ref, x_ref, acc_ref, *refs):
    left, right = refs[2:4]

    def halves(t):
        source, target = from_ref[t], to_ref[t]
        first = dot(left[t], x_ref[source], (1, 0)).astype(BF16)
        second = dot(left[t], x_ref[target], (0, 0)).astype(BF16)
        return t, source, target, first, second

    def add(t, source, target, first, second):
        acc_ref[target] += dot(first, right[t], (1, 1))
        acc_ref[source] += dot(second, right[t], (1, 0))

    @pl.loop(0, TERMS // STEP)
    def _(i):
        live = count_ref[0] - i * STEP
        for k in range(STEP // GROUP):
            @pl.when(live > k * GROUP)
            def _():
                for copy in term_copies(i * (STEP // GROUP) + k, *refs):
                    copy.wait()

        @pl.when(live >= STEP)
        def _():
            held = halves(i * STEP)
            for j in range(1, STEP):
                ahead = halves(i * STEP + j)
                add(*held)
                held = ahead
            add(*held)

        @pl.when((live > 0) & (live < STEP))
        def _():
            @pl.loop(0, live)
            def _(j):
                add(*halves(i * STEP + j))


def keep_copies(core, acc_ref, keep_ref, sems):
    return [
        pltpu.make_async_copy(
            acc_ref.at[:, block_rows(x, core), :], keep_ref.at[pl.ds(x * SEC, SEC)], sems.at[x]
        )
        for x in range(CHIPS_X)
    ]


def split_out(core, acc_ref, send, send_ref, sems):
    copies = []
    for x in range(CHIPS_X):
        @pl.loop(0, SEC)
        def _(s):
            send[x * SEC + s] = acc_ref[s, block_rows(x, 1 - core), :].astype(BF16)

        at = pl.ds(x * SEC, SEC)
        copies.append(pltpu.make_async_copy(send.at[at], send_ref.at[at], sems.at[CHIPS_X + x]))
        copies[-1].start()
    return copies


def total_of(terms):
    return lax.fori_loop(0, SEC, lambda s, total: total + fold(terms(s)), jnp.zeros((8, LANES), F32))


def first_kernel(count_ref, from_ref, to_ref, at_ref, own_ref, other_ref, left_ref, right_ref,
                 keep_ref, send_ref, sums_ref, norm_ref, start, x_ref, acc_ref, send, left, right, term_sems, sems):
    core = at_ref[0]
    gathers = [
        pltpu.make_async_copy(
            ref.at[:, pl.ds(x * ROWS, ROWS), :], start.at[:, block_rows(x, at), :], sems.at[2 * x + k]
        )
        for x in range(CHIPS_X) for k, (ref, at) in enumerate(((own_ref, core), (other_ref, 1 - core)))
    ]
    for copy in gathers:
        copy.start()
    start_terms(count_ref, left_ref, right_ref, left, right, term_sems)

    @pl.loop(0, SEC)
    def _(s):
        acc_ref[s] = jnp.zeros((B, B), F32)

    for copy in gathers:
        copy.wait()
    mean_sq = jnp.sum(total_of(lambda s: start[s] * start[s]), keepdims=True) / ENTRIES
    scale = 1.0 / jnp.sqrt(mean_sq + 1e-06)
    norm_ref[0] = jnp.broadcast_to(scale, (8, LANES))
    norm_ref[1] = jnp.broadcast_to(mean_sq, (8, LANES))

    @pl.loop(0, SEC)
    def _(s):
        x_ref[s] = (start[s] * scale).astype(BF16)

    apply_terms(count_ref, from_ref, to_ref, x_ref, acc_ref, left_ref, right_ref, left, right, term_sems)

    copies = keep_copies(core, acc_ref, keep_ref, sems)
    for copy in copies:
        copy.start()
    copies += split_out(core, acc_ref, send, send_ref, sems)
    sums_ref[0] = scale * total_of(lambda s: start[s] * acc_ref[s])
    for copy in copies:
        copy.wait()


def second_kernel(count_ref, from_ref, to_ref, at_ref, own_ref, other_ref, more_ref, left_ref, right_ref,
                  keep_ref, send_ref, sums_ref, mine_ref, x_ref, acc_ref, send, left, right, term_sems, sems):
    core = at_ref[0]
    gathers = [
        pltpu.make_async_copy(
            ref.at[pl.ds(x * SEC, SEC)], x_ref.at[:, block_rows(x, at), :], sems.at[2 * x + k]
        )
        for x in range(CHIPS_X) for k, (ref, at) in enumerate(((own_ref, core), (other_ref, 1 - core)))
    ]
    for copy in gathers:
        copy.start()
    start_terms(count_ref, left_ref, right_ref, left, right, term_sems)

    @pl.loop(0, SEC)
    def _(s):
        acc_ref[s] = jnp.zeros((B, B), F32)

    for copy in gathers:
        copy.wait()
    apply_terms(count_ref, from_ref, to_ref, x_ref, acc_ref, left_ref, right_ref, left, right, term_sems)

    copies = keep_copies(core, acc_ref, keep_ref, sems)
    for copy in copies:
        copy.start()
    copies += split_out(core, acc_ref, send, send_ref, sems)
    mine_ref[...] = x_ref[at_ref[1]].astype(F32)
    sums_ref[0] = total_of(lambda s: x_ref[s].astype(F32) * acc_ref[s])
    sums_ref[1:] = more_ref[...]
    for copy in copies:
        copy.wait()


def join_kernel(keep_ref, got_ref, sums_ref, got_sums_ref, out_ref):
    row = lax.broadcasted_iota(jnp.int32, (16, LANES), 0)
    tile = jnp.zeros((16, LANES), F32)
    for k in range(sums_ref.shape[0]):
        rest = jnp.sum(sums_ref[k] + got_sums_ref[k], keepdims=True)
        for part in range(3):
            top = rest.astype(BF16).astype(F32)
            tile = jnp.where(row == 3 * k + part, top, tile)
            rest = rest - top
    tile = tile.astype(BF16)

    @pl.loop(0, PIECES)
    def _(p):
        block = (keep_ref[p] + got_ref[p].astype(F32)).astype(BF16)
        out_ref[p, :ROWS, :] = block[:, :LANES]
        out_ref[p, ROWS:2 * ROWS, :] = block[:, LANES:]
        out_ref[p, 2 * ROWS:, :] = tile


def gathered_sum(got_ref, scalars):
    def add(p, total):
        return total + got_ref[p].astype(F32)

    total = lax.fori_loop(0, PIECES, add, jnp.zeros((2 * ROWS + 16, LANES), F32))
    row = lax.broadcasted_iota(jnp.int32, (16, LANES), 0)
    tile = total[2 * ROWS:, :]
    means = [
        jnp.sum(jnp.where((row >= 3 * k) & (row < 3 * k + 3), tile, 0.0), keepdims=True) / (LANES * ENTRIES)
        for k in range(scalars)
    ]
    return total[:2 * ROWS, :], means


def correct_kernel(got_ref, start_ref, diag_ref, norm_ref, copies_ref, sums_ref, corr_ref, sigma_ref, theta_ref):
    sigma, (theta,) = gathered_sum(got_ref, 1)
    vec = start_ref[...] * norm_ref[0, :1, :1]
    corr = (sigma - theta * vec) / jnp.maximum(jnp.abs(diag_ref[...] - theta), 1.0)
    sigma_ref[...] = sigma
    corr_ref[...] = corr
    theta_ref[...] = jnp.broadcast_to(theta, theta_ref.shape)
    for k, other in enumerate((vec, corr, sigma)):
        sums_ref[k] = fold(other * corr)
    rounded = corr.astype(BF16)

    @pl.loop(0, PIECES)
    def _(p):
        copies_ref[p, :, :LANES] = rounded[:ROWS, :]
        copies_ref[p, :, LANES:] = rounded[ROWS:, :]


def ritz_kernel(got_ref, start_ref, norm_ref, corr_ref, sigma_ref, theta_ref, out_ref, coef_ref):
    h_corr, (quad, along, corr_sq, cross) = gathered_sum(got_ref, 4)
    theta, scale, mean_sq = theta_ref[:1, :1], norm_ref[0, :1, :1], norm_ref[1, :1, :1]
    vec_sq = mean_sq * scale * scale
    ortho_sq = jnp.maximum(corr_sq - along * along * (2.0 - vec_sq), 0.0)
    inv = 1.0 / jnp.sqrt(ortho_sq + 1e-06)
    beta = (cross - along * theta) * inv
    gamma = (quad - 2.0 * along * cross + along * along * theta) * inv * inv
    lowest = 0.5 * (theta + gamma) - jnp.sqrt((0.5 * (theta - gamma)) ** 2 + beta * beta)
    norm = jnp.sqrt(beta * beta + (lowest - theta) ** 2)
    one, two = beta / norm, (lowest - theta) / norm
    coef_ref[0] = jnp.broadcast_to(scale * (one - two * along * inv), (8, LANES))
    coef_ref[1] = jnp.broadcast_to(two * inv, (8, LANES))
    vec, sigma = start_ref[...] * scale, sigma_ref[...]
    vec_two, sigma_two = (corr_ref[...] - along * vec) * inv, (h_corr - along * sigma) * inv
    resid = one * sigma + two * sigma_two - lowest * (one * vec + two * vec_two)
    for p in range(N_OP):
        out_ref[p, :, :LANES] = resid[:ROWS, :]
        out_ref[p, :, LANES:] = resid[ROWS:, :]


def shape(*dims, dtype=F32):
    return jax.ShapeDtypeStruct(dims, dtype)


SMEM = pl.BlockSpec(memory_space=pltpu.SMEM)
WHOLE = pl.BlockSpec(memory_space=pltpu.VMEM)
ANY = pl.BlockSpec(memory_space=pl.ANY)
TERM_SCRATCH = [
    pltpu.VMEM((SEC, B, B), BF16),
    pltpu.VMEM((SEC, B, B), F32),
    pltpu.VMEM((PIECES, ROWS, B), BF16),
    pltpu.VMEM((TERMS, B, B), BF16),
    pltpu.VMEM((TERMS, B, B), BF16),
    pltpu.SemaphoreType.DMA((2, TERMS // GROUP)),
    pltpu.SemaphoreType.DMA((2 * CHIPS_X,)),
]
SPLIT_SHAPES = [shape(PIECES, ROWS, B), shape(PIECES, ROWS, B, dtype=BF16)]


def call(kernel, mib, **kwargs):
    return pl.pallas_call(
        kernel, compiler_params=pltpu.CompilerParams(vmem_limit_bytes=mib << 20), name=kernel.__name__, **kwargs
    )


def swap(x):
    return lax.ppermute(x, "op", CORE_SWAP)


def exchange(x):
    return lax.all_to_all(x, ("op", "sec"), 0, 0, tiled=True, axis_index_groups=GROUPS)


def own_rows(block, op):
    rows = lax.dynamic_slice_in_dim(block, op * ROWS, ROWS, 0)
    return jnp.concatenate([rows[:, :LANES], rows[:, LANES:]], axis=0)


def reduce_partial(keep, send, sums):
    payload = call(
        join_kernel,
        16,
        out_shape=shape(PIECES, 2 * ROWS + 16, LANES, dtype=BF16),
        in_specs=[WHOLE] * 4,
        out_specs=WHOLE,
    )(keep, swap(send), sums, swap(sums))
    return exchange(payload)


def per_device(start_vector, diag_guess, left_env, right_env, sector_from, sector_to, term_count):
    op, sector = lax.axis_index("op"), lax.axis_index("sec")
    core = op % 2
    at = jnp.stack([core, sector]).astype(jnp.int32)
    terms = (term_count, sector_from, sector_to, at)

    mine = lax.dynamic_index_in_dim(start_vector.reshape(CHIPS_X, 2, ROWS, B), core, 1, keepdims=False)
    mine = jnp.broadcast_to(mine.reshape(1, B // 2, B), (SEC, B // 2, B))
    own = lax.all_to_all(mine, "sec", 0, 0, tiled=True)
    start, diag = own_rows(start_vector[0], op), own_rows(diag_guess[0], op)

    keep, send, sums, norm = call(
        first_kernel,
        32,
        out_shape=SPLIT_SHAPES + [shape(1, 8, LANES), shape(2, 8, LANES)],
        in_specs=[SMEM] * 4 + [ANY] * 4,
        out_specs=[ANY] * 2 + [WHOLE] * 2,
        scratch_shapes=[pltpu.VMEM((SEC, B, B), F32)] + TERM_SCRATCH,
    )(*terms, own, swap(own), left_env, right_env)

    got = reduce_partial(keep, send, sums)
    copies, more, corr, sigma, theta = call(
        correct_kernel,
        16,
        out_shape=[
            shape(PIECES, ROWS, B, dtype=BF16),
            shape(3, 8, LANES),
            shape(2 * ROWS, LANES),
            shape(2 * ROWS, LANES),
            shape(8, LANES),
        ],
        in_specs=[WHOLE] * 4,
        out_specs=[WHOLE] * 5,
    )(got, start, diag, norm)

    own = exchange(copies)
    keep, send, sums, corr_mine = call(
        second_kernel,
        28,
        out_shape=SPLIT_SHAPES + [shape(4, 8, LANES), shape(B, B)],
        in_specs=[SMEM] * 4 + [ANY] * 2 + [WHOLE] + [ANY] * 2,
        out_specs=[ANY] * 2 + [WHOLE] * 2,
        scratch_shapes=TERM_SCRATCH,
    )(*terms, own, swap(own), more, left_env, right_env)

    got = reduce_partial(keep, send, sums)
    resid, coefs = call(
        ritz_kernel,
        16,
        out_shape=[shape(N_OP, ROWS, B), shape(2, 8, LANES)],
        in_specs=[WHOLE] * 6,
        out_specs=[WHOLE] * 2,
    )(got, start, norm, corr, sigma, theta)

    ritz_residual = lax.all_to_all(resid, "op", 0, 0, tiled=True).reshape(1, B, B)
    ritz_vector = coefs[0, 0, 0] * start_vector + coefs[1, 0, 0] * corr_mine[None]
    return (ritz_vector, ritz_residual)


def solution(mesh):
    return jax.shard_map(
        per_device,
        mesh=mesh,
        in_specs=(
            P("sec", None, None),
            P("sec", None, None),
            P(("op", "sec"), None, None),
            P(("op", "sec"), None, None),
            P(("op", "sec")),
            P(("op", "sec")),
            P(("op", "sec")),
        ),
        out_specs=(P("sec", None, None), P("sec", None, None)),
        check_vma=False,
    )
```

```python
import jax
import jax.numpy as jnp
from jax import lax
from jax.experimental import pallas as pl
from jax.experimental.pallas import tpu as pltpu
from jax.sharding import PartitionSpec as P

F32, BF16 = jnp.float32, jnp.bfloat16
SEC, B, LANES = 16, 256, 128
HALF = B // 2
CHIPS_X, N_OP = 4, 8
TERMS, GROUP, STEP = 64, 8, 16
ENTRIES = SEC * B * B
CORE_SWAP = [(i, i ^ 1) for i in range(N_OP)]
ALONG_X = [[2 * x + core for x in range(CHIPS_X)] for core in range(2)]
SCALARS = 16


def dot(a, b, contract):
    return lax.dot_general(a, b, ((contract[:1], contract[1:]), ((), ())), preferred_element_type=F32)


def fold(block):
    block = jnp.sum(block.reshape(-1, 8, block.shape[-1]), axis=0)
    return sum(block[:, k:k + LANES] for k in range(0, block.shape[-1], LANES))


def half_rows(core):
    return pl.ds(pl.multiple_of(core * HALF, HALF), HALF)


def fold_columns(half):
    return jnp.concatenate([half[:, :LANES], half[:, LANES:]], axis=0)


def store_half(ref, at, columns):
    ref[at, :, :LANES] = columns[:HALF, :]
    ref[at, :, LANES:] = columns[HALF:, :]


def total_of(ref):
    return jnp.sum(ref, keepdims=True)


def square_kernel(start_ref, out_ref):
    squares = fold(start_ref[0] * start_ref[0])
    for s in range(SEC):
        out_ref[s] = squares


def scale_kernel(at_ref, got_ref, start_ref, copies_ref, sums_ref, start_half_ref, norm_ref):
    squares = got_ref[0]
    for s in range(1, SEC):
        squares = squares + got_ref[s]
    mean_sq = total_of(squares) / ENTRIES
    scale = 1.0 / jnp.sqrt(mean_sq + 1e-06)
    norm_ref[0] = jnp.broadcast_to(scale, (8, LANES))
    norm_ref[1] = jnp.broadcast_to(mean_sq, (8, LANES))
    start = start_ref[0, half_rows(at_ref[0]), :]
    start_half_ref[...] = fold_columns(start)
    vec = start * scale
    rounded = vec.astype(BF16)
    for s in range(SEC):
        copies_ref[s] = rounded
    wide = rounded.astype(F32)
    sums_ref[0] = fold(vec * wide) / CHIPS_X
    sums_ref[1] = fold(wide * wide) / CHIPS_X


def apply_kernel(count_ref, from_ref, to_ref, at_ref, own_ref, other_ref, more_ref, left_ref, right_ref,
                 keep_ref, send_ref, sums_ref, x_ref, acc_ref, send, left, right, term_sems, sems):
    core = at_ref[0]

    def term_copies(i):
        at = pl.ds(i * GROUP, GROUP)
        return (
            pltpu.make_async_copy(left_ref.at[at], left.at[at], term_sems.at[0, i]),
            pltpu.make_async_copy(right_ref.at[at], right.at[at], term_sems.at[1, i]),
        )

    gathers = [
        pltpu.make_async_copy(own_ref, x_ref.at[:, half_rows(core), :], sems.at[0]),
        pltpu.make_async_copy(other_ref, x_ref.at[:, half_rows(1 - core), :], sems.at[1]),
    ]
    for copy in gathers:
        copy.start()
    for i in range(TERMS // GROUP):
        @pl.when(i * GROUP < count_ref[0])
        def _():
            for copy in term_copies(i):
                copy.start()

    @pl.loop(0, SEC)
    def _(s):
        acc_ref[s] = jnp.zeros((B, B), F32)

    for copy in gathers:
        copy.wait()

    def halves(t):
        source, target = from_ref[t], to_ref[t]
        first = dot(left[t], x_ref[source], (1, 0)).astype(BF16)
        second = dot(left[t], x_ref[target], (0, 0)).astype(BF16)
        return t, source, target, first, second

    def add(t, source, target, first, second):
        acc_ref[target] += dot(first, right[t], (1, 1))
        acc_ref[source] += dot(second, right[t], (1, 0))

    @pl.loop(0, TERMS // STEP)
    def _(i):
        live = count_ref[0] - i * STEP
        for k in range(STEP // GROUP):
            @pl.when(live > k * GROUP)
            def _():
                for copy in term_copies(i * (STEP // GROUP) + k):
                    copy.wait()

        @pl.when(live >= STEP)
        def _():
            held = halves(i * STEP)
            for j in range(1, STEP):
                ahead = halves(i * STEP + j)
                add(*held)
                held = ahead
            add(*held)

        @pl.when((live > 0) & (live < STEP))
        def _():
            @pl.loop(0, live)
            def _(j):
                add(*halves(i * STEP + j))

    keep_copy = pltpu.make_async_copy(acc_ref.at[:, half_rows(core), :], keep_ref, sems.at[0])
    keep_copy.start()

    @pl.loop(0, SEC)
    def _(s):
        send[s] = acc_ref[s, half_rows(1 - core), :].astype(BF16)

    send_copy = pltpu.make_async_copy(send, send_ref, sems.at[1])
    send_copy.start()

    def inner(s, total):
        return total + fold(x_ref[s].astype(F32) * acc_ref[s])

    sums_ref[0] = lax.fori_loop(0, SEC, inner, jnp.zeros((8, LANES), F32))
    sums_ref[1:] = more_ref[...]
    keep_copy.wait()
    send_copy.wait()


def join_kernel(keep_ref, got_ref, sums_ref, got_sums_ref, out_ref):
    row = lax.broadcasted_iota(jnp.int32, (SCALARS, LANES), 0)
    lane = lax.broadcasted_iota(jnp.int32, (SCALARS, LANES), 1)
    tile = jnp.zeros((SCALARS, LANES), F32)
    for k in range(sums_ref.shape[0]):
        rest = total_of(sums_ref[k] + got_sums_ref[k])
        for part in range(3):
            top = rest.astype(BF16).astype(F32)
            tile = jnp.where((row == part) & (lane == k), top, tile)
            rest = rest - top
    tile = tile.astype(BF16)

    @pl.loop(0, SEC)
    def _(s):
        block = (keep_ref[s] + got_ref[s].astype(F32)).astype(BF16)
        out_ref[s, :HALF, :] = block[:, :LANES]
        out_ref[s, HALF:B, :] = block[:, LANES:]
        out_ref[s, B:, :] = tile


def sum_kernel(got_ref, out_ref):
    for k in range(0, B, HALF):
        total = got_ref[0, k:k + HALF, :].astype(F32)
        for s in range(1, SEC):
            total = total + got_ref[s, k:k + HALF, :].astype(F32)
        for x in range(CHIPS_X):
            out_ref[x, k:k + HALF, :] = total
    tile = got_ref[0, B:, :].astype(F32)
    for s in range(1, SEC):
        tile = tile + got_ref[s, B:, :].astype(F32)
    tile = tile[:8, :] + tile[8:, :]
    for x in range(CHIPS_X):
        out_ref[x, B:, :] = tile


def sum_of_chips(got_ref, scalars):
    total = got_ref[0]
    for x in range(1, CHIPS_X):
        total = total + got_ref[x]
    tile = total[B:, :]
    lane = lax.broadcasted_iota(jnp.int32, tile.shape, 1)
    means = [total_of(jnp.where(lane == k, tile, 0.0)) / ENTRIES for k in range(scalars)]
    return total[:B, :], means


def ratio(whole, part):
    return jnp.where(part > 0.0, whole / jnp.where(part > 0.0, part, 1.0), 1.0)


def correct_kernel(at_ref, got_ref, start_ref, diag_ref, norm_ref, copies_ref, sums_ref, corr_ref, sigma_ref, theta_ref):
    sigma, (theta, vec_round, round_sq) = sum_of_chips(got_ref, 3)
    theta = theta * ratio(vec_round, round_sq)
    vec = start_ref[...] * norm_ref[0, :1, :1]
    diag = fold_columns(diag_ref[0, half_rows(at_ref[0]), :])
    corr = (sigma - theta * vec) / jnp.maximum(jnp.abs(diag - theta), 1.0)
    sigma_ref[...] = sigma
    corr_ref[...] = corr
    theta_ref[...] = jnp.broadcast_to(theta, theta_ref.shape)
    rounded = corr.astype(BF16)
    for s in range(SEC):
        store_half(copies_ref, s, rounded)
    wide = rounded.astype(F32)
    pairs = ((vec, corr), (corr, corr), (sigma, corr), (corr, wide), (wide, wide))
    for k, (one, two) in enumerate(pairs):
        sums_ref[k] = fold(one * two) / CHIPS_X


def ritz_kernel(got_ref, start_ref, norm_ref, corr_ref, sigma_ref, theta_ref, out_ref):
    h_corr, (quad, along, corr_sq, cross, corr_round, round_sq) = sum_of_chips(got_ref, 6)
    theta, scale, mean_sq = theta_ref[:1, :1], norm_ref[0, :1, :1], norm_ref[1, :1, :1]
    quad = quad * ratio(corr_round, round_sq)
    vec_sq = mean_sq * scale * scale
    ortho_sq = jnp.maximum(corr_sq - along * along * (2.0 - vec_sq), 0.0)
    inv = 1.0 / jnp.sqrt(ortho_sq + 1e-06)
    beta = (cross - along * theta) * inv
    gamma = (quad - 2.0 * along * cross + along * along * theta) * inv * inv
    lowest = 0.5 * (theta + gamma) - jnp.sqrt((0.5 * (theta - gamma)) ** 2 + beta * beta)
    norm = jnp.sqrt(beta * beta + (lowest - theta) ** 2)
    one, two = beta / norm, (lowest - theta) / norm
    vec, sigma = start_ref[...] * scale, sigma_ref[...]
    vec_two, sigma_two = (corr_ref[...] - along * vec) * inv, (h_corr - along * sigma) * inv
    ritz = one * vec + two * vec_two
    store_half(out_ref, 0, ritz)
    store_half(out_ref, 1, one * sigma + two * sigma_two - lowest * ritz)


def place_kernel(at_ref, own_ref, other_ref, vector_ref, residual_ref):
    core = at_ref[0]
    for k, ref in enumerate((vector_ref, residual_ref)):
        ref[0, half_rows(core), :] = own_ref[k]
        ref[0, half_rows(1 - core), :] = other_ref[k]


def shape(*dims, dtype=F32):
    return jax.ShapeDtypeStruct(dims, dtype)


SMEM = pl.BlockSpec(memory_space=pltpu.SMEM)
WHOLE = pl.BlockSpec(memory_space=pltpu.VMEM)
ANY = pl.BlockSpec(memory_space=pl.ANY)
GATHER = shape(SEC, HALF, B, dtype=BF16)
COLUMNS = shape(B, LANES)


def call(kernel, mib, ins, outs, *args, **kwargs):
    return pl.pallas_call(
        kernel,
        out_shape=outs,
        in_specs=ins,
        compiler_params=pltpu.CompilerParams(vmem_limit_bytes=mib << 20),
        name=kernel.__name__,
        **kwargs,
    )(*args)


def swap(x):
    return lax.ppermute(x, "op", CORE_SWAP)


def over_sectors(x):
    return lax.all_to_all(x, "sec", 0, 0, tiled=True)


def apply_ham(terms, copies, more, left_env, right_env):
    own = over_sectors(copies)
    keep, send, sums = call(
        apply_kernel,
        58,
        [SMEM] * 4 + [ANY] * 2 + [WHOLE] + [ANY] * 2,
        [shape(SEC, HALF, B), GATHER, shape(more.shape[0] + 1, 8, LANES)],
        *terms, own, swap(own), more, left_env, right_env,
        out_specs=[ANY] * 2 + [WHOLE],
        scratch_shapes=[
            pltpu.VMEM((SEC, B, B), BF16),
            pltpu.VMEM((SEC, B, B), F32),
            pltpu.VMEM((SEC, HALF, B), BF16),
            pltpu.VMEM((TERMS, B, B), BF16),
            pltpu.VMEM((TERMS, B, B), BF16),
            pltpu.SemaphoreType.DMA((2, TERMS // GROUP)),
            pltpu.SemaphoreType.DMA((2,)),
        ],
    )
    payload = call(
        join_kernel, 16, [WHOLE] * 4, shape(SEC, B + SCALARS, LANES, dtype=BF16),
        keep, swap(send), sums, swap(sums),
    )
    chips = call(sum_kernel, 16, [WHOLE], shape(CHIPS_X, B + 8, LANES), over_sectors(payload))
    return lax.all_to_all(chips, "op", 0, 0, tiled=True, axis_index_groups=ALONG_X)


def per_device(start_vector, diag_guess, left_env, right_env, sector_from, sector_to, term_count):
    at = (lax.axis_index("op") % 2).astype(jnp.int32).reshape(1)
    terms = (term_count, sector_from, sector_to, at)
    squares = call(square_kernel, 16, [WHOLE], shape(SEC, 8, LANES), start_vector)
    copies, more, start, norm = call(
        scale_kernel, 16, [SMEM] + [WHOLE] * 2,
        [GATHER, shape(2, 8, LANES), COLUMNS, shape(2, 8, LANES)],
        at, over_sectors(squares), start_vector,
    )
    got = apply_ham(terms, copies, more, left_env, right_env)
    copies, more, corr, sigma, theta = call(
        correct_kernel, 16, [SMEM] + [WHOLE] * 4,
        [GATHER, shape(5, 8, LANES), COLUMNS, COLUMNS, shape(8, LANES)],
        at, got, start, diag_guess, norm,
    )
    got = apply_ham(terms, copies, more, left_env, right_env)
    halves = call(ritz_kernel, 16, [WHOLE] * 6, shape(2, HALF, B), got, start, norm, corr, sigma, theta)
    return call(
        place_kernel, 16, [SMEM] + [WHOLE] * 2, [shape(1, B, B), shape(1, B, B)], at, halves, swap(halves)
    )


def solution(mesh):
    return jax.shard_map(
        per_device,
        mesh=mesh,
        in_specs=(
            P("sec", None, None),
            P("sec", None, None),
            P(("op", "sec"), None, None),
            P(("op", "sec"), None, None),
            P(("op", "sec")),
            P(("op", "sec")),
            P(("op", "sec")),
        ),
        out_specs=(P("sec", None, None), P("sec", None, None)),
        check_vma=False,
    )
```

```python
import jax
import jax.numpy as jnp
from jax import lax
from jax.experimental import pallas as pl
from jax.experimental.pallas import tpu as pltpu
from jax.sharding import PartitionSpec as P

F32, BF16 = jnp.float32, jnp.bfloat16
SEC, B, LANES = 16, 256, 128
HALF = B // 2
CHIPS_X, N_OP = 4, 8
TERMS, GROUP, STEP, AHEAD = 64, 8, 16, 3
ENTRIES = SEC * B * B
CORE_SWAP = [(i, i ^ 1) for i in range(N_OP)]
ALONG_X = [[(i, (i + 2 * hops) % N_OP) for i in range(N_OP)] for hops in range(1, CHIPS_X)]
SCALARS = 16


def dot(a, b, contract):
    return lax.dot_general(a, b, ((contract[:1], contract[1:]), ((), ())), preferred_element_type=F32)


def fold(block):
    block = jnp.sum(block.reshape(-1, 8, block.shape[-1]), axis=0)
    return sum(block[:, k:k + LANES] for k in range(0, block.shape[-1], LANES))


def half_rows(core):
    return pl.ds(pl.multiple_of(core * HALF, HALF), HALF)


def fold_columns(half):
    return jnp.concatenate([half[:, :LANES], half[:, LANES:]], axis=0)


def store_half(ref, at, columns):
    ref[at, :, :LANES] = columns[:HALF, :]
    ref[at, :, LANES:] = columns[HALF:, :]


def total_of(ref):
    return jnp.sum(ref, keepdims=True)


def square_kernel(at_ref, start_ref, out_ref, half_ref):
    squares = fold(start_ref[0] * start_ref[0])
    for s in range(SEC):
        out_ref[s] = squares
    half_ref[...] = start_ref[0, half_rows(at_ref[0]), :]


def scale_kernel(got_ref, start_ref, copies_ref, sums_ref, start_half_ref, norm_ref):
    squares = got_ref[0]
    for s in range(1, SEC):
        squares = squares + got_ref[s]
    mean_sq = total_of(squares) / ENTRIES
    scale = 1.0 / jnp.sqrt(mean_sq + 1e-06)
    norm_ref[0] = jnp.broadcast_to(scale, (8, LANES))
    norm_ref[1] = jnp.broadcast_to(mean_sq, (8, LANES))
    start = start_ref[...]
    start_half_ref[...] = fold_columns(start)
    vec = start * scale
    rounded = vec.astype(BF16)
    for s in range(SEC):
        copies_ref[s] = rounded
    wide = rounded.astype(F32)
    sums_ref[0] = fold(vec * wide) / CHIPS_X
    sums_ref[1] = fold(wide * wide) / CHIPS_X


def apply_kernel(count_ref, from_ref, to_ref, at_ref, own_ref, other_ref, more_ref, left_ref, right_ref,
                 keep_ref, send_ref, sums_ref, *rest):
    core = at_ref[0]
    fetched = len(rest) > 4
    left, right = rest[:2] if fetched else (left_ref, right_ref)
    x_ref, acc_ref, send, sems = rest[2:6] if fetched else rest

    def term_copies(i):
        at = pl.ds(i * GROUP, GROUP)
        return [
            pltpu.make_async_copy(ref.at[at], held.at[at], rest[6].at[k, i])
            for k, (ref, held) in enumerate(((left_ref, left), (right_ref, right)))
        ]

    def fetch(i):
        @pl.when((i < TERMS // GROUP) & (i * GROUP < count_ref[0]))
        def _():
            for copy in term_copies(i):
                copy.start()

    gathers = [
        pltpu.make_async_copy(own_ref, x_ref.at[:, half_rows(core), :], sems.at[0]),
        pltpu.make_async_copy(other_ref, x_ref.at[:, half_rows(1 - core), :], sems.at[1]),
    ]
    for copy in gathers:
        copy.start()
    if fetched:
        for i in range(AHEAD):
            fetch(i)

    @pl.loop(0, SEC)
    def _(s):
        acc_ref[s] = jnp.zeros((B, B), F32)

    for copy in gathers:
        copy.wait()

    def halves(t):
        source, target = from_ref[t], to_ref[t]
        first = dot(left[t], x_ref[source], (1, 0)).astype(BF16)
        second = dot(left[t], x_ref[target], (0, 0)).astype(BF16)
        return t, source, target, first, second

    def add(t, source, target, first, second):
        acc_ref[target] += dot(first, right[t], (1, 1))
        acc_ref[source] += dot(second, right[t], (1, 0))

    @pl.loop(0, TERMS // STEP)
    def _(i):
        live = count_ref[0] - i * STEP
        for k in range(STEP // GROUP if fetched else 0):
            @pl.when(live > k * GROUP)
            def _():
                for copy in term_copies(i * (STEP // GROUP) + k):
                    copy.wait()

            fetch(i * (STEP // GROUP) + k + AHEAD)

        @pl.when(live >= STEP)
        def _():
            held = halves(i * STEP)
            for j in range(1, STEP):
                ahead = halves(i * STEP + j)
                add(*held)
                held = ahead
            add(*held)

        @pl.when((live > 0) & (live < STEP))
        def _():
            @pl.loop(0, live)
            def _(j):
                add(*halves(i * STEP + j))

    keep_copy = pltpu.make_async_copy(acc_ref.at[:, half_rows(core), :], keep_ref, sems.at[0])
    keep_copy.start()

    @pl.loop(0, SEC)
    def _(s):
        send[s] = acc_ref[s, half_rows(1 - core), :].astype(BF16)

    send_copy = pltpu.make_async_copy(send, send_ref, sems.at[1])
    send_copy.start()

    def inner(s, total):
        return total + fold(x_ref[s].astype(F32) * acc_ref[s])

    sums_ref[0] = lax.fori_loop(0, SEC, inner, jnp.zeros((8, LANES), F32))
    sums_ref[1:] = more_ref[...]
    keep_copy.wait()
    send_copy.wait()


def join_kernel(keep_ref, got_ref, sums_ref, got_sums_ref, out_ref):
    row = lax.broadcasted_iota(jnp.int32, (SCALARS, LANES), 0)
    lane = lax.broadcasted_iota(jnp.int32, (SCALARS, LANES), 1)
    tile = jnp.zeros((SCALARS, LANES), F32)
    for k in range(sums_ref.shape[0]):
        rest = total_of(sums_ref[k] + got_sums_ref[k])
        for part in range(3):
            top = rest.astype(BF16).astype(F32)
            tile = jnp.where((row == part) & (lane == k), top, tile)
            rest = rest - top
    tile = tile.astype(BF16)

    @pl.loop(0, SEC)
    def _(s):
        block = (keep_ref[s] + got_ref[s].astype(F32)).astype(BF16)
        out_ref[s, :HALF, :] = block[:, :LANES]
        out_ref[s, HALF:B, :] = block[:, LANES:]
        out_ref[s, B:, :] = tile


def sum_kernel(got_ref, out_ref):
    for k in range(0, B, HALF):
        total = got_ref[0, k:k + HALF, :].astype(F32)
        for s in range(1, SEC):
            total = total + got_ref[s, k:k + HALF, :].astype(F32)
        out_ref[k:k + HALF, :] = total
    tile = got_ref[0, B:, :].astype(F32)
    for s in range(1, SEC):
        tile = tile + got_ref[s, B:, :].astype(F32)
    out_ref[B:, :] = tile[:8, :] + tile[8:, :]


def sum_of_chips(part_refs, scalars):
    own, near, across, far = (ref[...] for ref in part_refs)
    total = (own + across) + (near + far)
    tile = total[B:, :]
    lane = lax.broadcasted_iota(jnp.int32, tile.shape, 1)
    means = [total_of(jnp.where(lane == k, tile, 0.0)) / ENTRIES for k in range(scalars)]
    return total[:B, :], means


def ratio(whole, part):
    return jnp.where(part > 0.0, whole / jnp.where(part > 0.0, part, 1.0), 1.0)


def correct_kernel(at_ref, own_ref, near_ref, across_ref, far_ref, start_ref, diag_ref, norm_ref, copies_ref, sums_ref, corr_ref, sigma_ref, theta_ref):
    sigma, (theta, vec_round, round_sq) = sum_of_chips((own_ref, near_ref, across_ref, far_ref), 3)
    theta = theta * ratio(vec_round, round_sq)
    vec = start_ref[...] * norm_ref[0, :1, :1]
    diag = fold_columns(diag_ref[0, half_rows(at_ref[0]), :])
    corr = (sigma - theta * vec) / jnp.maximum(jnp.abs(diag - theta), 1.0)
    sigma_ref[...] = sigma
    corr_ref[...] = corr
    theta_ref[...] = jnp.broadcast_to(theta, theta_ref.shape)
    rounded = corr.astype(BF16)
    for s in range(SEC):
        store_half(copies_ref, s, rounded)
    wide = rounded.astype(F32)
    pairs = ((vec, corr), (corr, corr), (sigma, corr), (corr, wide), (wide, wide))
    for k, (one, two) in enumerate(pairs):
        sums_ref[k] = fold(one * two) / CHIPS_X


def ritz_kernel(own_ref, near_ref, across_ref, far_ref, start_ref, norm_ref, corr_ref, sigma_ref, theta_ref, out_ref):
    h_corr, (quad, along, corr_sq, cross, corr_round, round_sq) = sum_of_chips((own_ref, near_ref, across_ref, far_ref), 6)
    theta, scale, mean_sq = theta_ref[:1, :1], norm_ref[0, :1, :1], norm_ref[1, :1, :1]
    quad = quad * ratio(corr_round, round_sq)
    vec_sq = mean_sq * scale * scale
    ortho_sq = jnp.maximum(corr_sq - along * along * (2.0 - vec_sq), 0.0)
    inv = 1.0 / jnp.sqrt(ortho_sq + 1e-06)
    beta = (cross - along * theta) * inv
    gamma = (quad - 2.0 * along * cross + along * along * theta) * inv * inv
    lowest = 0.5 * (theta + gamma) - jnp.sqrt((0.5 * (theta - gamma)) ** 2 + beta * beta)
    norm = jnp.sqrt(beta * beta + (lowest - theta) ** 2)
    one, two = beta / norm, (lowest - theta) / norm
    vec, sigma = start_ref[...] * scale, sigma_ref[...]
    vec_two, sigma_two = (corr_ref[...] - along * vec) * inv, (h_corr - along * sigma) * inv
    ritz = one * vec + two * vec_two
    store_half(out_ref, 0, ritz)
    store_half(out_ref, 1, one * sigma + two * sigma_two - lowest * ritz)


def place_kernel(at_ref, own_ref, other_ref, vector_ref, residual_ref):
    core = at_ref[0]
    for k, ref in enumerate((vector_ref, residual_ref)):
        ref[0, half_rows(core), :] = own_ref[k]
        ref[0, half_rows(1 - core), :] = other_ref[k]


def shape(*dims, dtype=F32):
    return jax.ShapeDtypeStruct(dims, dtype)


SMEM = pl.BlockSpec(memory_space=pltpu.SMEM)
WHOLE = pl.BlockSpec(memory_space=pltpu.VMEM)
ANY = pl.BlockSpec(memory_space=pl.ANY)
GATHER = shape(SEC, HALF, B, dtype=BF16)
COLUMNS = shape(B, LANES)


def call(kernel, mib, ins, outs, *args, **kwargs):
    return pl.pallas_call(
        kernel,
        out_shape=outs,
        in_specs=ins,
        compiler_params=pltpu.CompilerParams(vmem_limit_bytes=mib << 20),
        name=kernel.__name__,
        **kwargs,
    )(*args)


def swap(x):
    return lax.ppermute(x, "op", CORE_SWAP)


def over_sectors(x):
    return lax.all_to_all(x, "sec", 0, 0, tiled=True)


def apply_call(terms, own, other, more, left_env, right_env, fetch):
    if fetch:
        left_env, right_env = (pltpu.with_memory_space_constraint(x, pltpu.HBM) for x in (left_env, right_env))
    return call(
        apply_kernel,
        28,
        [SMEM] * 4 + [ANY] * 2 + [WHOLE] + [ANY if fetch else WHOLE] * 2,
        [shape(SEC, HALF, B), GATHER, shape(more.shape[0] + 1, 8, LANES)] + [shape(TERMS, B, B, dtype=BF16)] * (2 * fetch),
        *terms, own, other, more, left_env, right_env,
        out_specs=[ANY] * 2 + [WHOLE] * (3 if fetch else 1),
        scratch_shapes=[
            pltpu.VMEM((SEC, B, B), BF16),
            pltpu.VMEM((SEC, B, B), F32),
            pltpu.VMEM((SEC, HALF, B), BF16),
            pltpu.SemaphoreType.DMA((2,)),
        ] + [pltpu.SemaphoreType.DMA((2, TERMS // GROUP))] * fetch,
    )


def apply_ham(terms, copies, more, left_env, right_env, fetch):
    own = over_sectors(copies)
    keep, send, sums, *held = apply_call(terms, own, swap(own), more, left_env, right_env, fetch)
    payload = call(
        join_kernel, 16, [WHOLE] * 4, shape(SEC, B + SCALARS, LANES, dtype=BF16),
        keep, swap(send), sums, swap(sums),
    )
    part = call(sum_kernel, 16, [WHOLE], shape(B + 8, LANES), over_sectors(payload))
    return (part, *(lax.ppermute(part, "op", perm) for perm in ALONG_X)), held


def per_device(start_vector, diag_guess, left_env, right_env, sector_from, sector_to, term_count):
    at = (lax.axis_index("op") % 2).astype(jnp.int32).reshape(1)
    terms = (term_count, sector_from, sector_to, at)
    squares, half = call(
        square_kernel, 16, [SMEM, WHOLE], [shape(SEC, 8, LANES), shape(HALF, B)], at, start_vector
    )
    copies, more, start, norm = call(
        scale_kernel, 16, [WHOLE] * 2,
        [GATHER, shape(2, 8, LANES), COLUMNS, shape(2, 8, LANES)],
        over_sectors(squares), half,
    )
    got, held = apply_ham(terms, copies, more, left_env, right_env, True)
    copies, more, corr, sigma, theta = call(
        correct_kernel, 16, [SMEM] + [WHOLE] * 7,
        [GATHER, shape(5, 8, LANES), COLUMNS, COLUMNS, shape(8, LANES)],
        at, *got, start, diag_guess, norm,
    )
    got, _ = apply_ham(terms, copies, more, *held, False)
    halves = call(ritz_kernel, 16, [WHOLE] * 9, shape(2, HALF, B), *got, start, norm, corr, sigma, theta)
    return call(
        place_kernel, 16, [SMEM] + [WHOLE] * 2, [shape(1, B, B), shape(1, B, B)], at, halves, swap(halves)
    )


def solution(mesh):
    return jax.shard_map(
        per_device,
        mesh=mesh,
        in_specs=(
            P("sec", None, None),
            P("sec", None, None),
            P(("op", "sec"), None, None),
            P(("op", "sec"), None, None),
            P(("op", "sec")),
            P(("op", "sec")),
            P(("op", "sec")),
        ),
        out_specs=(P("sec", None, None), P("sec", None, None)),
        check_vma=False,
    )
```

```python
import jax
import jax.numpy as jnp
from jax import lax
from jax.experimental import pallas as pl
from jax.experimental.pallas import tpu as pltpu
from jax.sharding import PartitionSpec as P

F32, BF16 = jnp.float32, jnp.bfloat16
SEC, B, LANES = 16, 256, 128
HALF = B // 2
CHIPS_X, N_OP = 4, 8
TERMS, GROUP, STEP, AHEAD = 64, 8, 16, 2
GROUPS = TERMS // GROUP - STEP // GROUP
ENTRIES = SEC * B * B
CORE_SWAP = [(i, i ^ 1) for i in range(N_OP)]
ALONG_X = [[(i, (i + 2 * hops) % N_OP) for i in range(N_OP)] for hops in range(1, CHIPS_X)]
SCALARS = 16


def dot(a, b, contract):
    return lax.dot_general(a, b, ((contract[:1], contract[1:]), ((), ())), preferred_element_type=F32)


def fold(block):
    block = jnp.sum(block.reshape(-1, 8, block.shape[-1]), axis=0)
    return sum(block[:, k:k + LANES] for k in range(0, block.shape[-1], LANES))


def half_rows(core):
    return pl.ds(pl.multiple_of(core * HALF, HALF), HALF)


def fold_columns(half):
    return jnp.concatenate([half[:, :LANES], half[:, LANES:]], axis=0)


def store_half(ref, at, columns):
    ref[at, :, :LANES] = columns[:HALF, :]
    ref[at, :, LANES:] = columns[HALF:, :]


def total_of(ref):
    return jnp.sum(ref, keepdims=True)


def square_kernel(at_ref, start_ref, out_ref, half_ref, start, sem):
    copy = pltpu.make_async_copy(start_ref, start, sem)
    copy.start()
    copy.wait()
    squares = fold(start[0] * start[0])
    for s in range(SEC):
        out_ref[s] = squares
    half_ref[...] = start[0, half_rows(at_ref[0]), :]


def scale_kernel(got_ref, start_ref, copies_ref, sums_ref, start_half_ref, norm_ref):
    squares = got_ref[0]
    for s in range(1, SEC):
        squares = squares + got_ref[s]
    mean_sq = total_of(squares) / ENTRIES
    scale = 1.0 / jnp.sqrt(mean_sq + 1e-06)
    norm_ref[0] = jnp.broadcast_to(scale, (8, LANES))
    norm_ref[1] = jnp.broadcast_to(mean_sq, (8, LANES))
    start = start_ref[...]
    start_half_ref[...] = fold_columns(start)
    vec = start * scale
    rounded = vec.astype(BF16)
    for s in range(SEC):
        copies_ref[s] = rounded
    wide = rounded.astype(F32)
    sums_ref[0] = fold(vec * wide) / CHIPS_X
    sums_ref[1] = fold(wide * wide) / CHIPS_X


def head_kernel(left_ref, right_ref, left_out, right_out, sems):
    copies = [
        pltpu.make_async_copy(ref.at[pl.ds(0, STEP)], out, sems.at[k])
        for k, (ref, out) in enumerate(((left_ref, left_out), (right_ref, right_out)))
    ]
    for copy in copies:
        copy.start()
    for copy in copies:
        copy.wait()


def apply_kernel(count_ref, from_ref, to_ref, at_ref, own_ref, other_ref, more_ref, left_head, right_head,
                 left_ref, right_ref, keep_ref, send_ref, sums_ref, *rest):
    core = at_ref[0]
    fetched = len(rest) > 4
    left, right = rest[:2] if fetched else (left_ref, right_ref)
    x_ref, acc_ref, halves_ref, sems = rest[2:6] if fetched else rest

    def term_copies(i):
        out = pl.ds(i * GROUP, GROUP)
        at = pl.ds(STEP + i * GROUP, GROUP)
        return [
            pltpu.make_async_copy(ref.at[at], held.at[out], rest[6].at[k, i])
            for k, (ref, held) in enumerate(((left_ref, left), (right_ref, right)))
        ]

    def fetch(i):
        @pl.when((i < GROUPS) & (STEP + i * GROUP < count_ref[0]))
        def _():
            for copy in term_copies(i):
                copy.start()

    gathers = [
        pltpu.make_async_copy(own_ref, x_ref.at[:, half_rows(core), :], sems.at[0]),
        pltpu.make_async_copy(other_ref, x_ref.at[:, half_rows(1 - core), :], sems.at[1]),
    ]
    for copy in gathers:
        copy.start()
    if fetched:
        for i in range(AHEAD):
            fetch(i)

    @pl.loop(0, SEC)
    def _(s):
        acc_ref[s] = jnp.zeros((B, B), F32)

    for copy in gathers:
        copy.wait()

    def step(i, lefts, rights, base):
        live = count_ref[0] - i * STEP

        def first_half(j):
            t = i * STEP + j
            block = lefts[base + j]
            halves_ref[2 * j] = dot(block, x_ref[from_ref[t]], (1, 0)).astype(BF16)
            halves_ref[2 * j + 1] = dot(block, x_ref[to_ref[t]], (0, 0)).astype(BF16)

        def second_half(j):
            t = i * STEP + j
            block = rights[base + j]
            acc_ref[to_ref[t]] += dot(halves_ref[2 * j], block, (1, 1))
            acc_ref[from_ref[t]] += dot(halves_ref[2 * j + 1], block, (1, 0))

        @pl.when(live >= STEP)
        def _():
            for j in range(STEP):
                first_half(j)
            for j in range(STEP):
                second_half(j)

        @pl.when((live > 0) & (live < STEP))
        def _():
            @pl.loop(0, live)
            def _(j):
                first_half(j)
                second_half(j)

    step(0, left_head, right_head, 0)

    @pl.loop(0, TERMS // STEP - 1)
    def _(i):
        for k in range(STEP // GROUP if fetched else 0):
            @pl.when(count_ref[0] > (i + 1) * STEP + k * GROUP)
            def _():
                for copy in term_copies(i * (STEP // GROUP) + k):
                    copy.wait()

            fetch(i * (STEP // GROUP) + k + AHEAD)

        step(i + 1, left, right, i * STEP)

    keep_copy = pltpu.make_async_copy(acc_ref.at[:, half_rows(core), :], keep_ref, sems.at[0])
    keep_copy.start()

    def inner(s, total):
        mine, theirs = half_rows(core), half_rows(1 - core)
        part = acc_ref[s, theirs, :]
        send_ref[s] = part.astype(BF16)
        total = total + fold(x_ref[s, theirs, :].astype(F32) * part)
        return total + fold(x_ref[s, mine, :].astype(F32) * acc_ref[s, mine, :])

    sums_ref[0] = lax.fori_loop(0, SEC, inner, jnp.zeros((8, LANES), F32))
    sums_ref[1:] = more_ref[...]
    keep_copy.wait()


def join_kernel(keep_ref, got_ref, sums_ref, got_sums_ref, out_ref):
    row = lax.broadcasted_iota(jnp.int32, (SCALARS, LANES), 0)
    lane = lax.broadcasted_iota(jnp.int32, (SCALARS, LANES), 1)
    tile = jnp.zeros((SCALARS, LANES), F32)
    for k in range(sums_ref.shape[0]):
        rest = total_of(sums_ref[k] + got_sums_ref[k])
        for part in range(3):
            top = rest.astype(BF16).astype(F32)
            tile = jnp.where((row == part) & (lane == k), top, tile)
            rest = rest - top
    tile = tile.astype(BF16)

    @pl.loop(0, SEC)
    def _(s):
        block = (keep_ref[s] + got_ref[s].astype(F32)).astype(BF16)
        out_ref[s, :HALF, :] = block[:, :LANES]
        out_ref[s, HALF:B, :] = block[:, LANES:]
        out_ref[s, B:, :] = tile


def sum_kernel(got_ref, out_ref):
    for k in range(0, B, HALF):
        total = got_ref[0, k:k + HALF, :].astype(F32)
        for s in range(1, SEC):
            total = total + got_ref[s, k:k + HALF, :].astype(F32)
        out_ref[k:k + HALF, :] = total
    tile = got_ref[0, B:, :].astype(F32)
    for s in range(1, SEC):
        tile = tile + got_ref[s, B:, :].astype(F32)
    out_ref[B:, :] = tile[:8, :] + tile[8:, :]


def sum_of_chips(part_refs, scalars):
    own, near, across, far = (ref[...] for ref in part_refs)
    total = (own + across) + (near + far)
    tile = total[B:, :]
    lane = lax.broadcasted_iota(jnp.int32, tile.shape, 1)
    means = [total_of(jnp.where(lane == k, tile, 0.0)) / ENTRIES for k in range(scalars)]
    return total[:B, :], means


def ratio(whole, part):
    return jnp.where(part > 0.0, whole / jnp.where(part > 0.0, part, 1.0), 1.0)


def correct_kernel(at_ref, own_ref, near_ref, across_ref, far_ref, start_ref, diag_ref, norm_ref, copies_ref, sums_ref, corr_ref, sigma_ref, theta_ref):
    sigma, (theta, vec_round, round_sq) = sum_of_chips((own_ref, near_ref, across_ref, far_ref), 3)
    theta = theta * ratio(vec_round, round_sq)
    vec = start_ref[...] * norm_ref[0, :1, :1]
    diag = fold_columns(diag_ref[0, half_rows(at_ref[0]), :])
    corr = (sigma - theta * vec) / jnp.maximum(jnp.abs(diag - theta), 1.0)
    sigma_ref[...] = sigma
    corr_ref[...] = corr
    theta_ref[...] = jnp.broadcast_to(theta, theta_ref.shape)
    rounded = corr.astype(BF16)
    for s in range(SEC):
        store_half(copies_ref, s, rounded)
    wide = rounded.astype(F32)
    pairs = ((vec, corr), (corr, corr), (sigma, corr), (corr, wide), (wide, wide))
    for k, (one, two) in enumerate(pairs):
        sums_ref[k] = fold(one * two) / CHIPS_X


def ritz_kernel(own_ref, near_ref, across_ref, far_ref, start_ref, norm_ref, corr_ref, sigma_ref, theta_ref, out_ref):
    h_corr, (quad, along, corr_sq, cross, corr_round, round_sq) = sum_of_chips((own_ref, near_ref, across_ref, far_ref), 6)
    theta, scale, mean_sq = theta_ref[:1, :1], norm_ref[0, :1, :1], norm_ref[1, :1, :1]
    quad = quad * ratio(corr_round, round_sq)
    vec_sq = mean_sq * scale * scale
    ortho_sq = jnp.maximum(corr_sq - along * along * (2.0 - vec_sq), 0.0)
    inv = 1.0 / jnp.sqrt(ortho_sq + 1e-06)
    beta = (cross - along * theta) * inv
    gamma = (quad - 2.0 * along * cross + along * along * theta) * inv * inv
    lowest = 0.5 * (theta + gamma) - jnp.sqrt((0.5 * (theta - gamma)) ** 2 + beta * beta)
    norm = jnp.sqrt(beta * beta + (lowest - theta) ** 2)
    one, two = beta / norm, (lowest - theta) / norm
    vec, sigma = start_ref[...] * scale, sigma_ref[...]
    vec_two, sigma_two = (corr_ref[...] - along * vec) * inv, (h_corr - along * sigma) * inv
    ritz = one * vec + two * vec_two
    store_half(out_ref, 0, ritz)
    store_half(out_ref, 1, one * sigma + two * sigma_two - lowest * ritz)


def place_kernel(at_ref, own_ref, other_ref, vector_ref, residual_ref):
    core = at_ref[0]
    for k, ref in enumerate((vector_ref, residual_ref)):
        ref[0, half_rows(core), :] = own_ref[k]
        ref[0, half_rows(1 - core), :] = other_ref[k]


def shape(*dims, dtype=F32):
    return jax.ShapeDtypeStruct(dims, dtype)


SMEM = pl.BlockSpec(memory_space=pltpu.SMEM)
WHOLE = pl.BlockSpec(memory_space=pltpu.VMEM)
ANY = pl.BlockSpec(memory_space=pl.ANY)
GATHER = shape(SEC, HALF, B, dtype=BF16)
COLUMNS = shape(B, LANES)


def call(kernel, mib, ins, outs, *args, **kwargs):
    return pl.pallas_call(
        kernel,
        out_shape=outs,
        in_specs=ins,
        compiler_params=pltpu.CompilerParams(vmem_limit_bytes=mib << 20),
        name=kernel.__name__,
        **kwargs,
    )(*args)


def swap(x):
    return lax.ppermute(x, "op", CORE_SWAP)


def over_sectors(x):
    return lax.all_to_all(x, "sec", 0, 0, tiled=True)


def in_hbm(*arrays):
    return [pltpu.with_memory_space_constraint(x, pltpu.HBM) for x in arrays]


def terms_shape(count):
    return [shape(count, B, B, dtype=BF16)] * 2


def apply_ham(terms, copies, more, head, left, right, fetch):
    own = over_sectors(copies)
    keep, send, sums, *held = call(
        apply_kernel,
        28,
        [SMEM] * 4 + [ANY] * 2 + [WHOLE] * 3 + [ANY if fetch else WHOLE] * 2,
        [shape(SEC, HALF, B), GATHER, shape(more.shape[0] + 1, 8, LANES)] + terms_shape(TERMS - STEP) * fetch,
        *terms, own, swap(own), more, *head, left, right,
        out_specs=[ANY] + [WHOLE] * (4 if fetch else 2),
        scratch_shapes=[
            pltpu.VMEM((SEC, B, B), BF16),
            pltpu.VMEM((SEC, B, B), F32),
            pltpu.VMEM((2 * STEP, B, B), BF16),
            pltpu.SemaphoreType.DMA((2,)),
        ] + [pltpu.SemaphoreType.DMA((2, GROUPS))] * fetch,
    )
    payload = call(
        join_kernel, 16, [WHOLE] * 4, shape(SEC, B + SCALARS, LANES, dtype=BF16),
        keep, swap(send), sums, swap(sums),
    )
    part = call(sum_kernel, 16, [WHOLE], shape(B + 8, LANES), over_sectors(payload))
    return (part, *(lax.ppermute(part, "op", perm) for perm in ALONG_X)), held


def per_device(start_vector, diag_guess, left_env, right_env, sector_from, sector_to, term_count):
    at = (lax.axis_index("op") % 2).astype(jnp.int32).reshape(1)
    terms = (term_count, sector_from, sector_to, at)
    squares, half = call(
        square_kernel, 16, [SMEM, ANY], [shape(SEC, 8, LANES), shape(HALF, B)], at, *in_hbm(start_vector),
        scratch_shapes=[pltpu.VMEM((1, B, B), F32), pltpu.SemaphoreType.DMA],
    )
    copies, more, start, norm = call(
        scale_kernel, 16, [WHOLE] * 2,
        [GATHER, shape(2, 8, LANES), COLUMNS, shape(2, 8, LANES)],
        over_sectors(squares), half,
    )
    far = in_hbm(left_env, right_env)
    head = call(
        head_kernel, 16, [ANY] * 2, terms_shape(STEP), *far,
        out_specs=[WHOLE] * 2, scratch_shapes=[pltpu.SemaphoreType.DMA((2,))],
    )
    got, held = apply_ham(terms, copies, more, head, *far, True)
    copies, more, corr, sigma, theta = call(
        correct_kernel, 16, [SMEM] + [WHOLE] * 7,
        [GATHER, shape(5, 8, LANES), COLUMNS, COLUMNS, shape(8, LANES)],
        at, *got, start, diag_guess, norm,
    )
    got, _ = apply_ham(terms, copies, more, head, *held, False)
    halves = call(ritz_kernel, 16, [WHOLE] * 9, shape(2, HALF, B), *got, start, norm, corr, sigma, theta)
    return call(
        place_kernel, 16, [SMEM] + [WHOLE] * 2, [shape(1, B, B), shape(1, B, B)], at, halves, swap(halves)
    )


def solution(mesh):
    return jax.shard_map(
        per_device,
        mesh=mesh,
        in_specs=(
            P("sec", None, None),
            P("sec", None, None),
            P(("op", "sec"), None, None),
            P(("op", "sec"), None, None),
            P(("op", "sec")),
            P(("op", "sec")),
            P(("op", "sec")),
        ),
        out_specs=(P("sec", None, None), P("sec", None, None)),
        check_vma=False,
    )
```

```python
import jax
import jax.numpy as jnp
from jax import lax
from jax.experimental import pallas as pl
from jax.experimental.pallas import tpu as pltpu
from jax.sharding import PartitionSpec as P

F32, BF16 = jnp.float32, jnp.bfloat16
SEC, B, LANES = 16, 256, 128
HALF = B // 2
CHIPS_X, N_OP = 4, 8
TERMS, GROUP, STEP, AHEAD = 64, 8, 16, 2
GROUPS = TERMS // GROUP - STEP // GROUP
ENTRIES = SEC * B * B
CORE_SWAP = [(i, i ^ 1) for i in range(N_OP)]
ALONG_X = [[(i, (i + 2 * hops) % N_OP) for i in range(N_OP)] for hops in range(1, CHIPS_X)]


def dot(a, b, contract):
    return lax.dot_general(a, b, ((contract[:1], contract[1:]), ((), ())), preferred_element_type=F32)


def fold(block):
    block = jnp.sum(block.reshape(-1, 8, block.shape[-1]), axis=0)
    return sum(block[:, k:k + LANES] for k in range(0, block.shape[-1], LANES))


def half_rows(core):
    return pl.ds(pl.multiple_of(core * HALF, HALF), HALF)


def fold_columns(half):
    return jnp.concatenate([half[:, :LANES], half[:, LANES:]], axis=0)


def store_half(ref, at, columns):
    ref[at, :, :LANES] = columns[:HALF, :]
    ref[at, :, LANES:] = columns[HALF:, :]


def total_of(ref):
    return jnp.sum(ref, keepdims=True)


def ratio(whole, part):
    return jnp.where(part > 0.0, whole / jnp.where(part > 0.0, part, 1.0), 1.0)


def over_rows(places):
    return jnp.broadcast_to(places, (B // 8, 8, LANES)).reshape(B, LANES)


def as_codes(values):
    return values.astype(jnp.int32).astype(jnp.int16)


def exponent_of(values):
    return jnp.ceil(jnp.log2(jnp.maximum(jnp.abs(values), 1e-30)) + 0.001)


def encode(half):
    exponent = exponent_of(jnp.max(jnp.abs(half).reshape(B // 8, 8, LANES), axis=0)) - 15.0
    codes = jnp.round(half * over_rows(jnp.exp2(-exponent)))
    return as_codes(jnp.clip(codes, -32767.0, 32767.0)), exponent


def encode_kernel(at_ref, start_ref, codes_ref, half_ref, start, sem):
    copy = pltpu.make_async_copy(start_ref, start, sem)
    copy.start()
    copy.wait()
    half = fold_columns(start[0, half_rows(at_ref[0]), :])
    half_ref[...] = half
    codes, exponent = encode(half)
    tail = as_codes(jnp.concatenate([exponent, jnp.zeros((8, LANES), F32)], axis=0))
    for s in range(SEC):
        codes_ref[s, :B, :] = codes
        codes_ref[s, B:, :] = tail


def decode(ref, s):
    exponent = ref[s, B:, :].astype(jnp.int32).astype(F32)[:8, :]
    return ref[s, :B, :].astype(jnp.int32).astype(F32) * over_rows(jnp.exp2(exponent))


def decode_start(core, own_ref, other_ref, x_ref, norm_ref):
    zero = jnp.zeros((8, LANES), F32)

    def squares(s, total):
        for ref in (own_ref, other_ref):
            block = decode(ref, s)
            total = total + fold(block * block)
        return total

    mean_sq = total_of(lax.fori_loop(0, SEC, squares, zero)) / ENTRIES
    scale = 1.0 / jnp.sqrt(mean_sq + 1e-06)
    norm_ref[0] = jnp.broadcast_to(scale, (8, LANES))
    norm_ref[1] = jnp.broadcast_to(mean_sq, (8, LANES))

    def place(s, totals):
        vec_round, round_sq = totals
        for ref, at in ((own_ref, core), (other_ref, 1 - core)):
            vec = decode(ref, s) * scale
            rounded = vec.astype(BF16)
            x_ref[s, half_rows(at), :LANES] = rounded[:HALF, :]
            x_ref[s, half_rows(at), LANES:] = rounded[HALF:, :]
            wide = rounded.astype(F32)
            vec_round, round_sq = vec_round + fold(vec * wide), round_sq + fold(wide * wide)
        return vec_round, round_sq

    vec_round, round_sq = lax.fori_loop(0, SEC, place, (zero, zero))
    return ratio(total_of(vec_round), total_of(round_sq))


def head_kernel(left_ref, right_ref, left_out, right_out, sems):
    copies = [
        pltpu.make_async_copy(ref.at[pl.ds(0, STEP)], out, sems.at[k])
        for k, (ref, out) in enumerate(((left_ref, left_out), (right_ref, right_out)))
    ]
    for copy in copies:
        copy.start()
    for copy in copies:
        copy.wait()


def first_kernel(count_ref, from_ref, to_ref, at_ref, own_ref, other_ref, left_head, right_head, left_ref, right_ref,
                 keep_ref, send_ref, sums_ref, norm_ref, left, right, x_ref, acc_ref, halves_ref, sems, term_sems):
    def prepare(core):
        return decode_start(core, own_ref, other_ref, x_ref, norm_ref)

    apply_terms(
        prepare, (count_ref, from_ref, to_ref, at_ref), (left_head, right_head), (left_ref, right_ref), (left, right),
        keep_ref, send_ref, sums_ref, x_ref, acc_ref, halves_ref, sems, term_sems,
    )


def second_kernel(count_ref, from_ref, to_ref, at_ref, own_ref, other_ref, more_ref, left_head, right_head,
                  left, right, keep_ref, send_ref, sums_ref, x_ref, acc_ref, halves_ref, sems):
    def prepare(core):
        copies = [
            pltpu.make_async_copy(own_ref, x_ref.at[:, half_rows(core), :], sems.at[0]),
            pltpu.make_async_copy(other_ref, x_ref.at[:, half_rows(1 - core), :], sems.at[1]),
        ]
        for copy in copies:
            copy.start()
        sums_ref[1:] = more_ref[...]
        for copy in copies:
            copy.wait()
        return 1.0

    apply_terms(
        prepare, (count_ref, from_ref, to_ref, at_ref), (left_head, right_head), None, (left, right),
        keep_ref, send_ref, sums_ref, x_ref, acc_ref, halves_ref, sems, None,
    )


def apply_terms(prepare, terms, heads, far, held, keep_ref, send_ref, sums_ref, x_ref, acc_ref, halves_ref, sems,
                term_sems):
    count_ref, from_ref, to_ref, at_ref = terms
    core = at_ref[0]

    def term_copies(i):
        out = pl.ds(i * GROUP, GROUP)
        at = pl.ds(STEP + i * GROUP, GROUP)
        return [
            pltpu.make_async_copy(ref.at[at], to.at[out], term_sems.at[k, i])
            for k, (ref, to) in enumerate(zip(far, held))
        ]

    def fetch(i):
        @pl.when((i < GROUPS) & (STEP + i * GROUP < count_ref[0]))
        def _():
            for copy in term_copies(i):
                copy.start()

    if far:
        for i in range(AHEAD):
            fetch(i)

    @pl.loop(0, SEC)
    def _(s):
        acc_ref[s] = jnp.zeros((B, B), F32)

    weight = prepare(core)

    def step(i, lefts, rights, base):
        live = count_ref[0] - i * STEP

        def first_half(j):
            t = i * STEP + j
            block = lefts[base + j]
            halves_ref[2 * j] = dot(block, x_ref[from_ref[t]], (1, 0)).astype(BF16)
            halves_ref[2 * j + 1] = dot(block, x_ref[to_ref[t]], (0, 0)).astype(BF16)

        def second_half(j):
            t = i * STEP + j
            block = rights[base + j]
            acc_ref[to_ref[t]] += dot(halves_ref[2 * j], block, (1, 1))
            acc_ref[from_ref[t]] += dot(halves_ref[2 * j + 1], block, (1, 0))

        @pl.when(live >= STEP)
        def _():
            for j in range(STEP):
                first_half(j)
            for j in range(STEP):
                second_half(j)

        @pl.when((live > 0) & (live < STEP))
        def _():
            @pl.loop(0, live)
            def _(j):
                first_half(j)
                second_half(j)

    step(0, *heads, 0)

    @pl.loop(0, TERMS // STEP - 1)
    def _(i):
        for k in range(STEP // GROUP if far else 0):
            @pl.when(count_ref[0] > (i + 1) * STEP + k * GROUP)
            def _():
                for copy in term_copies(i * (STEP // GROUP) + k):
                    copy.wait()

            fetch(i * (STEP // GROUP) + k + AHEAD)

        step(i + 1, *held, i * STEP)

    keep_copy = pltpu.make_async_copy(acc_ref.at[:, half_rows(core), :], keep_ref, sems.at[0])
    keep_copy.start()

    def inner(s, total):
        mine, theirs = half_rows(core), half_rows(1 - core)
        part = acc_ref[s, theirs, :]
        send_ref[s] = part.astype(BF16)
        total = total + fold(x_ref[s, theirs, :].astype(F32) * part)
        return total + fold(x_ref[s, mine, :].astype(F32) * acc_ref[s, mine, :])

    sums_ref[0] = lax.fori_loop(0, SEC, inner, jnp.zeros((8, LANES), F32)) * weight
    keep_copy.wait()


def join_kernel(keep_ref, got_ref, sums_ref, got_sums_ref, out_ref):
    lane = lax.broadcasted_iota(jnp.int32, (8, LANES), 1)
    scalars = jnp.zeros((8, LANES), F32)
    for k in range(sums_ref.shape[0]):
        scalars = jnp.where(lane == k, total_of(sums_ref[k] + got_sums_ref[k]), scalars)
    power = exponent_of(scalars)
    scaled = scalars * jnp.exp2(14.0 - power)
    high = jnp.round(scaled)
    low = jnp.round((scaled - high) * 32768.0)
    row = lax.broadcasted_iota(jnp.int32, (8, LANES), 0)
    lower = jnp.where(row == 0, high, jnp.where(row == 1, low, jnp.where(row == 2, power, 0.0)))

    @pl.loop(0, SEC, unroll=4)
    def _(s):
        codes, exponent = encode(fold_columns(keep_ref[s] + got_ref[s].astype(F32)))
        out_ref[s, :B, :] = codes
        out_ref[s, B:, :] = as_codes(jnp.concatenate([exponent, lower], axis=0))


def sum_kernel(got_ref, out_ref):
    def add(s, totals):
        tail = got_ref[s, B:, :].astype(jnp.int32).astype(F32)
        scalars = (tail[8:9, :] + tail[9:10, :] * (1.0 / 32768.0)) * jnp.exp2(tail[10:11, :] - 14.0)
        return totals[0] + decode(got_ref, s), totals[1] + scalars

    zeros = jnp.zeros((B, LANES), F32), jnp.zeros((1, LANES), F32)
    total, scalars = lax.fori_loop(0, SEC, add, zeros, unroll=4)
    out_ref[:B, :] = total
    row = lax.broadcasted_iota(jnp.int32, (8, LANES), 0)
    out_ref[B:, :] = jnp.where(row == 0, jnp.broadcast_to(scalars, (8, LANES)), 0.0)


def sum_of_chips(part_refs, scalars):
    own, near, across, far = (ref[...] for ref in part_refs)
    total = (own + across) + (near + far)
    tile = total[B:, :]
    lane = lax.broadcasted_iota(jnp.int32, tile.shape, 1)
    means = [total_of(jnp.where(lane == k, tile, 0.0)) / ENTRIES for k in range(scalars)]
    return total[:B, :], means


def correct_kernel(at_ref, own_ref, near_ref, across_ref, far_ref, start_ref, diag_ref, norm_ref, copies_ref, sums_ref, corr_ref, sigma_ref, theta_ref):
    sigma, (theta,) = sum_of_chips((own_ref, near_ref, across_ref, far_ref), 1)
    vec = start_ref[...] * norm_ref[0, :1, :1]
    diag = fold_columns(diag_ref[0, half_rows(at_ref[0]), :])
    corr = (sigma - theta * vec) / jnp.maximum(jnp.abs(diag - theta), 1.0)
    sigma_ref[...] = sigma
    corr_ref[...] = corr
    theta_ref[...] = jnp.broadcast_to(theta, theta_ref.shape)
    rounded = corr.astype(BF16)
    for s in range(SEC):
        store_half(copies_ref, s, rounded)
    wide = rounded.astype(F32)
    pairs = ((vec, corr), (corr, corr), (sigma, corr), (corr, wide), (wide, wide))
    for k, (one, two) in enumerate(pairs):
        sums_ref[k] = fold(one * two) / CHIPS_X


def ritz_kernel(own_ref, near_ref, across_ref, far_ref, start_ref, norm_ref, corr_ref, sigma_ref, theta_ref, out_ref):
    h_corr, (quad, along, corr_sq, cross, corr_round, round_sq) = sum_of_chips((own_ref, near_ref, across_ref, far_ref), 6)
    theta, scale, mean_sq = theta_ref[:1, :1], norm_ref[0, :1, :1], norm_ref[1, :1, :1]
    quad = quad * ratio(corr_round, round_sq)
    vec_sq = mean_sq * scale * scale
    ortho_sq = jnp.maximum(corr_sq - along * along * (2.0 - vec_sq), 0.0)
    inv = 1.0 / jnp.sqrt(ortho_sq + 1e-06)
    beta = (cross - along * theta) * inv
    gamma = (quad - 2.0 * along * cross + along * along * theta) * inv * inv
    lowest = 0.5 * (theta + gamma) - jnp.sqrt((0.5 * (theta - gamma)) ** 2 + beta * beta)
    norm = jnp.sqrt(beta * beta + (lowest - theta) ** 2)
    one, two = beta / norm, (lowest - theta) / norm
    vec, sigma = start_ref[...] * scale, sigma_ref[...]
    vec_two, sigma_two = (corr_ref[...] - along * vec) * inv, (h_corr - along * sigma) * inv
    ritz = one * vec + two * vec_two
    store_half(out_ref, 0, ritz)
    store_half(out_ref, 1, one * sigma + two * sigma_two - lowest * ritz)


def place_kernel(at_ref, own_ref, other_ref, vector_ref, residual_ref):
    core = at_ref[0]
    for k, ref in enumerate((vector_ref, residual_ref)):
        ref[0, half_rows(core), :] = own_ref[k]
        ref[0, half_rows(1 - core), :] = other_ref[k]


def shape(*dims, dtype=F32):
    return jax.ShapeDtypeStruct(dims, dtype)


SMEM = pl.BlockSpec(memory_space=pltpu.SMEM)
WHOLE = pl.BlockSpec(memory_space=pltpu.VMEM)
ANY = pl.BlockSpec(memory_space=pl.ANY)
GATHER = shape(SEC, HALF, B, dtype=BF16)
COLUMNS = shape(B, LANES)
PIECES = shape(SEC, B + 16, LANES, dtype=jnp.int16)


def call(kernel, mib, ins, outs, *args, **kwargs):
    return pl.pallas_call(
        kernel,
        out_shape=outs,
        in_specs=ins,
        compiler_params=pltpu.CompilerParams(vmem_limit_bytes=mib << 20),
        name=kernel.__name__,
        **kwargs,
    )(*args)


def swap(x):
    return lax.ppermute(x, "op", CORE_SWAP)


def over_sectors(x):
    return lax.all_to_all(x, "sec", 0, 0, tiled=True)


def in_hbm(*arrays):
    return [pltpu.with_memory_space_constraint(x, pltpu.HBM) for x in arrays]


def terms_shape(count):
    return [shape(count, B, B, dtype=BF16)] * 2


APPLY_SCRATCH = [
    pltpu.VMEM((SEC, B, B), BF16),
    pltpu.VMEM((SEC, B, B), F32),
    pltpu.VMEM((2 * STEP, B, B), BF16),
    pltpu.SemaphoreType.DMA((2,)),
]
SPLIT = [shape(SEC, HALF, B), GATHER]


def reduce_partial(keep, send, sums):
    payload = call(
        join_kernel, 16, [WHOLE] * 4, PIECES,
        keep, swap(send), sums, swap(sums),
    )
    part = call(sum_kernel, 16, [WHOLE], shape(B + 8, LANES), over_sectors(payload))
    return part, *(lax.ppermute(part, "op", perm) for perm in ALONG_X)


def per_device(start_vector, diag_guess, left_env, right_env, sector_from, sector_to, term_count):
    at = (lax.axis_index("op") % 2).astype(jnp.int32).reshape(1)
    terms = (term_count, sector_from, sector_to, at)
    codes, start = call(
        encode_kernel, 16, [SMEM, ANY], [PIECES, COLUMNS],
        at, *in_hbm(start_vector),
        scratch_shapes=[pltpu.VMEM((1, B, B), F32), pltpu.SemaphoreType.DMA],
    )
    far = in_hbm(left_env, right_env)
    head = call(
        head_kernel, 16, [ANY] * 2, terms_shape(STEP), *far,
        out_specs=[WHOLE] * 2, scratch_shapes=[pltpu.SemaphoreType.DMA((2,))],
    )
    own = over_sectors(codes)
    keep, send, sums, norm, *held = call(
        first_kernel, 28, [SMEM] * 4 + [WHOLE] * 4 + [ANY] * 2,
        SPLIT + [shape(1, 8, LANES), shape(2, 8, LANES)] + terms_shape(TERMS - STEP),
        *terms, own, swap(own), *head, *far,
        out_specs=[ANY] + [WHOLE] * 5,
        scratch_shapes=APPLY_SCRATCH + [pltpu.SemaphoreType.DMA((2, GROUPS))],
    )
    got = reduce_partial(keep, send, sums)
    copies, more, corr, sigma, theta = call(
        correct_kernel, 16, [SMEM] + [WHOLE] * 7,
        [GATHER, shape(5, 8, LANES), COLUMNS, COLUMNS, shape(8, LANES)],
        at, *got, start, diag_guess, norm,
    )
    own = over_sectors(copies)
    keep, send, sums = call(
        second_kernel, 28, [SMEM] * 4 + [ANY] * 2 + [WHOLE] * 5,
        SPLIT + [shape(6, 8, LANES)],
        *terms, own, swap(own), more, *head, *held,
        out_specs=[ANY] + [WHOLE] * 2,
        scratch_shapes=APPLY_SCRATCH,
    )
    got = reduce_partial(keep, send, sums)
    halves = call(ritz_kernel, 16, [WHOLE] * 9, shape(2, HALF, B), *got, start, norm, corr, sigma, theta)
    return call(
        place_kernel, 16, [SMEM] + [WHOLE] * 2, [shape(1, B, B), shape(1, B, B)], at, halves, swap(halves)
    )


def solution(mesh):
    return jax.shard_map(
        per_device,
        mesh=mesh,
        in_specs=(
            P("sec", None, None),
            P("sec", None, None),
            P(("op", "sec"), None, None),
            P(("op", "sec"), None, None),
            P(("op", "sec")),
            P(("op", "sec")),
            P(("op", "sec")),
        ),
        out_specs=(P("sec", None, None), P("sec", None, None)),
        check_vma=False,
    )
```

```python
import jax
import jax.numpy as jnp
from jax import lax
from jax.experimental import pallas as pl
from jax.experimental.pallas import tpu as pltpu
from jax.sharding import PartitionSpec as P

F32, BF16 = jnp.float32, jnp.bfloat16
SEC, B, LANES = 16, 256, 128
HALF = B // 2
CHIPS_X, N_OP = 4, 8
TERMS, GROUP, STEP, AHEAD = 64, 8, 16, 2
GROUPS = TERMS // GROUP - STEP // GROUP
ENTRIES = SEC * B * B
CORE_SWAP = [(i, i ^ 1) for i in range(N_OP)]
ALONG_X = [[(i, (i + 2 * hops) % N_OP) for i in range(N_OP)] for hops in range(1, CHIPS_X)]


def dot(a, b, contract):
    return lax.dot_general(a, b, ((contract[:1], contract[1:]), ((), ())), preferred_element_type=F32)


def fold(block):
    block = jnp.sum(block.reshape(-1, 8, block.shape[-1]), axis=0)
    return sum(block[:, k:k + LANES] for k in range(0, block.shape[-1], LANES))


def half_rows(core):
    return pl.ds(pl.multiple_of(core * HALF, HALF), HALF)


def fold_columns(half):
    return jnp.concatenate([half[:, :LANES], half[:, LANES:]], axis=0)


def store_half(ref, at, columns):
    ref[at, :, :LANES] = columns[:HALF, :]
    ref[at, :, LANES:] = columns[HALF:, :]


def total_of(ref):
    return jnp.sum(ref, keepdims=True)


def ratio(whole, part):
    return jnp.where(part > 0.0, whole / jnp.where(part > 0.0, part, 1.0), 1.0)


def over_rows(places):
    return jnp.broadcast_to(places, (B // 8, 8, LANES)).reshape(B, LANES)


def as_codes(values):
    return values.astype(jnp.int32).astype(jnp.int16)


def exponent_of(values):
    return jnp.ceil(jnp.log2(jnp.maximum(jnp.abs(values), 1e-30)) + 0.001)


def encode(half):
    exponent = exponent_of(jnp.max(jnp.abs(half).reshape(B // 8, 8, LANES), axis=0)) - 15.0
    codes = jnp.round(half * over_rows(jnp.exp2(-exponent)))
    return as_codes(jnp.clip(codes, -32767.0, 32767.0)), exponent


def encode_kernel(at_ref, start_ref, codes_ref, half_ref, start, sem):
    copy = pltpu.make_async_copy(start_ref, start, sem)
    copy.start()
    copy.wait()
    half = fold_columns(start[0, half_rows(at_ref[0]), :])
    half_ref[...] = half
    codes, exponent = encode(half)
    tail = as_codes(jnp.concatenate([exponent, jnp.zeros((8, LANES), F32)], axis=0))
    for s in range(SEC):
        codes_ref[s, :B, :] = codes
        codes_ref[s, B:, :] = tail


def decode(piece):
    exponent = piece[B:, :].astype(jnp.int32).astype(F32)[:8, :]
    return piece[:B, :].astype(jnp.int32).astype(F32) * over_rows(jnp.exp2(exponent))


def decode_start(core, own_ref, other_ref, x_ref, norm_ref):
    zero = jnp.zeros((8, LANES), F32)

    def squares(s, total):
        for ref in (own_ref, other_ref):
            block = decode(ref.at[s])
            total = total + fold(block * block)
        return total

    mean_sq = total_of(lax.fori_loop(0, SEC, squares, zero, unroll=4)) / ENTRIES
    scale = 1.0 / jnp.sqrt(mean_sq + 1e-06)
    norm_ref[0] = jnp.broadcast_to(scale, (8, LANES))
    norm_ref[1] = jnp.broadcast_to(mean_sq, (8, LANES))

    def place(s, totals):
        vec_round, round_sq = totals
        for ref, at in ((own_ref, core), (other_ref, 1 - core)):
            vec = decode(ref.at[s]) * scale
            rounded = vec.astype(BF16)
            x_ref[s, half_rows(at), :LANES] = rounded[:HALF, :]
            x_ref[s, half_rows(at), LANES:] = rounded[HALF:, :]
            wide = rounded.astype(F32)
            vec_round, round_sq = vec_round + fold(vec * wide), round_sq + fold(wide * wide)
        return vec_round, round_sq

    vec_round, round_sq = lax.fori_loop(0, SEC, place, (zero, zero), unroll=2)
    return ratio(total_of(vec_round), total_of(round_sq))


def head_kernel(left_ref, right_ref, left_out, right_out, sems):
    copies = [
        pltpu.make_async_copy(ref.at[pl.ds(0, STEP)], out, sems.at[k])
        for k, (ref, out) in enumerate(((left_ref, left_out), (right_ref, right_out)))
    ]
    for copy in copies:
        copy.start()
    for copy in copies:
        copy.wait()


def first_kernel(count_ref, from_ref, to_ref, at_ref, own_ref, other_ref, left_head, right_head, left_ref, right_ref,
                 keep_ref, send_ref, sums_ref, norm_ref, left, right, x_ref, acc_ref, halves_ref, sems, term_sems):
    def prepare(core):
        return decode_start(core, own_ref, other_ref, x_ref, norm_ref)

    apply_terms(
        prepare, (count_ref, from_ref, to_ref, at_ref), (left_head, right_head), (left_ref, right_ref), (left, right),
        keep_ref, send_ref, sums_ref, x_ref, acc_ref, halves_ref, sems, term_sems,
    )


def second_kernel(count_ref, from_ref, to_ref, at_ref, own_ref, other_ref, more_ref, left_head, right_head,
                  left, right, keep_ref, send_ref, sums_ref, x_ref, acc_ref, halves_ref, sems):
    def prepare(core):
        copies = [
            pltpu.make_async_copy(own_ref, x_ref.at[:, half_rows(core), :], sems.at[0]),
            pltpu.make_async_copy(other_ref, x_ref.at[:, half_rows(1 - core), :], sems.at[1]),
        ]
        for copy in copies:
            copy.start()
        sums_ref[1:] = more_ref[...]
        for copy in copies:
            copy.wait()
        return 1.0

    apply_terms(
        prepare, (count_ref, from_ref, to_ref, at_ref), (left_head, right_head), None, (left, right),
        keep_ref, send_ref, sums_ref, x_ref, acc_ref, halves_ref, sems, None,
    )


def apply_terms(prepare, terms, heads, far, held, keep_ref, send_ref, sums_ref, x_ref, acc_ref, halves_ref, sems,
                term_sems):
    count_ref, from_ref, to_ref, at_ref = terms
    core = at_ref[0]

    def term_copies(i):
        out = pl.ds(i * GROUP, GROUP)
        at = pl.ds(STEP + i * GROUP, GROUP)
        return [
            pltpu.make_async_copy(ref.at[at], to.at[out], term_sems.at[k, i])
            for k, (ref, to) in enumerate(zip(far, held))
        ]

    def fetch(i):
        @pl.when((i < GROUPS) & (STEP + i * GROUP < count_ref[0]))
        def _():
            for copy in term_copies(i):
                copy.start()

    if far:
        for i in range(AHEAD):
            fetch(i)

    @pl.loop(0, SEC)
    def _(s):
        acc_ref[s] = jnp.zeros((B, B), F32)

    weight = prepare(core)

    def step(i, lefts, rights, base):
        live = count_ref[0] - i * STEP

        def first_half(j):
            t = i * STEP + j
            block = lefts[base + j]
            halves_ref[2 * j] = dot(block, x_ref[from_ref[t]], (1, 0)).astype(BF16)
            halves_ref[2 * j + 1] = dot(block, x_ref[to_ref[t]], (0, 0)).astype(BF16)

        def second_half(j):
            t = i * STEP + j
            block = rights[base + j]
            acc_ref[to_ref[t]] += dot(halves_ref[2 * j], block, (1, 1))
            acc_ref[from_ref[t]] += dot(halves_ref[2 * j + 1], block, (1, 0))

        @pl.when(live >= STEP)
        def _():
            for j in range(STEP):
                first_half(j)
            for j in range(STEP):
                second_half(j)

        @pl.when((live > 0) & (live < STEP))
        def _():
            @pl.loop(0, live)
            def _(j):
                first_half(j)
                second_half(j)

    step(0, *heads, 0)

    @pl.loop(0, TERMS // STEP - 1)
    def _(i):
        for k in range(STEP // GROUP if far else 0):
            @pl.when(count_ref[0] > (i + 1) * STEP + k * GROUP)
            def _():
                for copy in term_copies(i * (STEP // GROUP) + k):
                    copy.wait()

            fetch(i * (STEP // GROUP) + k + AHEAD)

        step(i + 1, *held, i * STEP)

    keep_copy = pltpu.make_async_copy(acc_ref.at[:, half_rows(core), :], keep_ref, sems.at[0])
    keep_copy.start()

    def inner(s, total):
        mine, theirs = half_rows(core), half_rows(1 - core)
        part = acc_ref[s, theirs, :]
        send_ref[s] = part.astype(BF16)
        total = total + fold(x_ref[s, theirs, :].astype(F32) * part)
        return total + fold(x_ref[s, mine, :].astype(F32) * acc_ref[s, mine, :])

    sums_ref[0] = lax.fori_loop(0, SEC, inner, jnp.zeros((8, LANES), F32)) * weight
    keep_copy.wait()


def scalar_rows(scalars):
    power = exponent_of(scalars)
    scaled = scalars * jnp.exp2(14.0 - power)
    high = jnp.round(scaled)
    low = jnp.round((scaled - high) * 32768.0)
    row = lax.broadcasted_iota(jnp.int32, (8, LANES), 0)
    return jnp.where(row == 0, high, jnp.where(row == 1, low, jnp.where(row == 2, power, 0.0)))


def store_piece(ref, half, rows):
    codes, exponent = encode(half)
    ref[:B, :] = codes
    ref[B:, :] = as_codes(jnp.concatenate([exponent, rows], axis=0))


def load_piece(ref):
    tail = ref[B:, :].astype(jnp.int32).astype(F32)
    scalars = (tail[8:9, :] + tail[9:10, :] * (1.0 / 32768.0)) * jnp.exp2(tail[10:11, :] - 14.0)
    return decode(ref), scalars


def join_kernel(keep_ref, got_ref, sums_ref, got_sums_ref, out_ref):
    lane = lax.broadcasted_iota(jnp.int32, (8, LANES), 1)
    scalars = jnp.zeros((8, LANES), F32)
    for k in range(sums_ref.shape[0]):
        scalars = jnp.where(lane == k, total_of(sums_ref[k] + got_sums_ref[k]), scalars)
    rows = scalar_rows(scalars)

    @pl.loop(0, SEC, unroll=4)
    def _(s):
        store_piece(out_ref.at[s], fold_columns(keep_ref[s] + got_ref[s].astype(F32)), rows)


def sum_kernel(got_ref, out_ref):
    def add(s, totals):
        half, scalars = load_piece(got_ref.at[s])
        return totals[0] + half, totals[1] + scalars

    zeros = jnp.zeros((B, LANES), F32), jnp.zeros((1, LANES), F32)
    half, scalars = lax.fori_loop(0, SEC, add, zeros, unroll=4)
    store_piece(out_ref, half, scalar_rows(jnp.broadcast_to(scalars, (8, LANES))))


def sum_of_chips(part_refs, count):
    own, near, across, far = (load_piece(ref) for ref in part_refs)
    half, scalars = ((own[k] + across[k]) + (near[k] + far[k]) for k in range(2))
    lane = lax.broadcasted_iota(jnp.int32, scalars.shape, 1)
    return half, [total_of(jnp.where(lane == k, scalars, 0.0)) / ENTRIES for k in range(count)]


def correct_kernel(at_ref, own_ref, near_ref, across_ref, far_ref, start_ref, diag_ref, norm_ref, copies_ref, sums_ref, corr_ref, sigma_ref, theta_ref):
    sigma, (theta,) = sum_of_chips((own_ref, near_ref, across_ref, far_ref), 1)
    vec = start_ref[...] * norm_ref[0, :1, :1]
    diag = fold_columns(diag_ref[0, half_rows(at_ref[0]), :])
    corr = (sigma - theta * vec) / jnp.maximum(jnp.abs(diag - theta), 1.0)
    sigma_ref[...] = sigma
    corr_ref[...] = corr
    theta_ref[...] = jnp.broadcast_to(theta, theta_ref.shape)
    rounded = corr.astype(BF16)
    for s in range(SEC):
        store_half(copies_ref, s, rounded)
    wide = rounded.astype(F32)
    pairs = ((vec, corr), (corr, corr), (sigma, corr), (corr, wide), (wide, wide))
    for k, (one, two) in enumerate(pairs):
        sums_ref[k] = fold(one * two) / CHIPS_X


def ritz_kernel(own_ref, near_ref, across_ref, far_ref, start_ref, norm_ref, corr_ref, sigma_ref, theta_ref, out_ref):
    h_corr, (quad, along, corr_sq, cross, corr_round, round_sq) = sum_of_chips((own_ref, near_ref, across_ref, far_ref), 6)
    theta, scale, mean_sq = theta_ref[:1, :1], norm_ref[0, :1, :1], norm_ref[1, :1, :1]
    quad = quad * ratio(corr_round, round_sq)
    vec_sq = mean_sq * scale * scale
    ortho_sq = jnp.maximum(corr_sq - along * along * (2.0 - vec_sq), 0.0)
    inv = 1.0 / jnp.sqrt(ortho_sq + 1e-06)
    beta = (cross - along * theta) * inv
    gamma = (quad - 2.0 * along * cross + along * along * theta) * inv * inv
    lowest = 0.5 * (theta + gamma) - jnp.sqrt((0.5 * (theta - gamma)) ** 2 + beta * beta)
    norm = jnp.sqrt(beta * beta + (lowest - theta) ** 2)
    one, two = beta / norm, (lowest - theta) / norm
    vec, sigma = start_ref[...] * scale, sigma_ref[...]
    vec_two, sigma_two = (corr_ref[...] - along * vec) * inv, (h_corr - along * sigma) * inv
    ritz = one * vec + two * vec_two
    store_half(out_ref, 0, ritz)
    store_half(out_ref, 1, one * sigma + two * sigma_two - lowest * ritz)


def place_kernel(at_ref, own_ref, other_ref, vector_ref, residual_ref):
    core = at_ref[0]
    for k, ref in enumerate((vector_ref, residual_ref)):
        ref[0, half_rows(core), :] = own_ref[k]
        ref[0, half_rows(1 - core), :] = other_ref[k]


def shape(*dims, dtype=F32):
    return jax.ShapeDtypeStruct(dims, dtype)


SMEM = pl.BlockSpec(memory_space=pltpu.SMEM)
WHOLE = pl.BlockSpec(memory_space=pltpu.VMEM)
ANY = pl.BlockSpec(memory_space=pl.ANY)
GATHER = shape(SEC, HALF, B, dtype=BF16)
COLUMNS = shape(B, LANES)
PIECES = shape(SEC, B + 16, LANES, dtype=jnp.int16)


def call(kernel, mib, ins, outs, *args, **kwargs):
    return pl.pallas_call(
        kernel,
        out_shape=outs,
        in_specs=ins,
        compiler_params=pltpu.CompilerParams(vmem_limit_bytes=mib << 20),
        name=kernel.__name__,
        **kwargs,
    )(*args)


def swap(x):
    return lax.ppermute(x, "op", CORE_SWAP)


def over_sectors(x):
    return lax.all_to_all(x, "sec", 0, 0, tiled=True)


def in_hbm(*arrays):
    return [pltpu.with_memory_space_constraint(x, pltpu.HBM) for x in arrays]


def terms_shape(count):
    return [shape(count, B, B, dtype=BF16)] * 2


APPLY_SCRATCH = [
    pltpu.VMEM((SEC, B, B), BF16),
    pltpu.VMEM((SEC, B, B), F32),
    pltpu.VMEM((2 * STEP, B, B), BF16),
    pltpu.SemaphoreType.DMA((2,)),
]
SPLIT = [shape(SEC, HALF, B), GATHER]


def reduce_partial(keep, send, sums):
    payload = call(
        join_kernel, 16, [WHOLE] * 4, PIECES,
        keep, swap(send), sums, swap(sums),
    )
    part = call(sum_kernel, 16, [WHOLE], shape(B + 16, LANES, dtype=jnp.int16), over_sectors(payload))
    return part, *(lax.ppermute(part, "op", perm) for perm in ALONG_X)


def per_device(start_vector, diag_guess, left_env, right_env, sector_from, sector_to, term_count):
    at = (lax.axis_index("op") % 2).astype(jnp.int32).reshape(1)
    terms = (term_count, sector_from, sector_to, at)
    codes, start = call(
        encode_kernel, 16, [SMEM, ANY], [PIECES, COLUMNS],
        at, *in_hbm(start_vector),
        scratch_shapes=[pltpu.VMEM((1, B, B), F32), pltpu.SemaphoreType.DMA],
    )
    far = in_hbm(left_env, right_env)
    head = call(
        head_kernel, 16, [ANY] * 2, terms_shape(STEP), *far,
        out_specs=[WHOLE] * 2, scratch_shapes=[pltpu.SemaphoreType.DMA((2,))],
    )
    own = over_sectors(codes)
    keep, send, sums, norm, *held = call(
        first_kernel, 28, [SMEM] * 4 + [WHOLE] * 4 + [ANY] * 2,
        SPLIT + [shape(1, 8, LANES), shape(2, 8, LANES)] + terms_shape(TERMS - STEP),
        *terms, own, swap(own), *head, *far,
        out_specs=[ANY] + [WHOLE] * 5,
        scratch_shapes=APPLY_SCRATCH + [pltpu.SemaphoreType.DMA((2, GROUPS))],
    )
    got = reduce_partial(keep, send, sums)
    copies, more, corr, sigma, theta = call(
        correct_kernel, 16, [SMEM] + [WHOLE] * 7,
        [GATHER, shape(5, 8, LANES), COLUMNS, COLUMNS, shape(8, LANES)],
        at, *got, start, diag_guess, norm,
    )
    own = over_sectors(copies)
    keep, send, sums = call(
        second_kernel, 28, [SMEM] * 4 + [ANY] * 2 + [WHOLE] * 5,
        SPLIT + [shape(6, 8, LANES)],
        *terms, own, swap(own), more, *head, *held,
        out_specs=[ANY] + [WHOLE] * 2,
        scratch_shapes=APPLY_SCRATCH,
    )
    got = reduce_partial(keep, send, sums)
    halves = call(ritz_kernel, 16, [WHOLE] * 9, shape(2, HALF, B), *got, start, norm, corr, sigma, theta)
    return call(
        place_kernel, 16, [SMEM] + [WHOLE] * 2, [shape(1, B, B), shape(1, B, B)], at, halves, swap(halves)
    )


def solution(mesh):
    return jax.shard_map(
        per_device,
        mesh=mesh,
        in_specs=(
            P("sec", None, None),
            P("sec", None, None),
            P(("op", "sec"), None, None),
            P(("op", "sec"), None, None),
            P(("op", "sec")),
            P(("op", "sec")),
            P(("op", "sec")),
        ),
        out_specs=(P("sec", None, None), P("sec", None, None)),
        check_vma=False,
    )
```

```python
import jax
import jax.numpy as jnp
from jax import lax
from jax.experimental import pallas as pl
from jax.experimental.pallas import tpu as pltpu
from jax.sharding import PartitionSpec as P

F32, BF16 = jnp.float32, jnp.bfloat16
SEC, B, LANES = 16, 256, 128
HALF = B // 2
CHIPS_X, N_OP = 4, 8
TERMS, GROUP, STEP, AHEAD = 64, 8, 16, 2
GROUPS = TERMS // GROUP - STEP // GROUP
ENTRIES = SEC * B * B
CORE_SWAP = [(i, i ^ 1) for i in range(N_OP)]
ALONG_X = [[(i, (i + 2 * hops) % N_OP) for i in range(N_OP)] for hops in range(1, CHIPS_X)]


def dot(a, b, contract):
    return lax.dot_general(a, b, ((contract[:1], contract[1:]), ((), ())), preferred_element_type=F32)


def fold(block):
    block = jnp.sum(block.reshape(-1, 8, block.shape[-1]), axis=0)
    return sum(block[:, k:k + LANES] for k in range(0, block.shape[-1], LANES))


def half_rows(core):
    return pl.ds(pl.multiple_of(core * HALF, HALF), HALF)


def fold_columns(half):
    return jnp.concatenate([half[:, :LANES], half[:, LANES:]], axis=0)


def store_half(ref, at, columns):
    ref[at, :, :LANES] = columns[:HALF, :]
    ref[at, :, LANES:] = columns[HALF:, :]


def total_of(ref):
    return jnp.sum(ref, keepdims=True)


def ratio(whole, part):
    return jnp.where(part > 0.0, whole / jnp.where(part > 0.0, part, 1.0), 1.0)


def over_rows(places):
    return jnp.broadcast_to(places, (B // 8, 8, LANES)).reshape(B, LANES)


def as_codes(values):
    return values.astype(jnp.int32).astype(jnp.int16)


def exponent_of(values):
    return jnp.ceil(jnp.log2(jnp.maximum(jnp.abs(values), 1e-30)) + 0.001)


def encode(half):
    exponent = exponent_of(jnp.max(jnp.abs(half).reshape(B // 8, 8, LANES), axis=0)) - 15.0
    codes = jnp.round(half * over_rows(jnp.exp2(-exponent)))
    return as_codes(jnp.clip(codes, -32767.0, 32767.0)), exponent


def decode(piece):
    exponent = piece[B:, :].astype(jnp.int32).astype(F32)[:8, :]
    return piece[:B, :].astype(jnp.int32).astype(F32) * over_rows(jnp.exp2(exponent))


def scalar_rows(scalars):
    power = exponent_of(scalars)
    scaled = scalars * jnp.exp2(14.0 - power)
    high = jnp.round(scaled)
    low = jnp.round((scaled - high) * 32768.0)
    row = lax.broadcasted_iota(jnp.int32, (8, LANES), 0)
    return jnp.where(row == 0, high, jnp.where(row == 1, low, jnp.where(row == 2, power, 0.0)))


def store_piece(ref, half, rows):
    codes, exponent = encode(half)
    ref[:B, :] = codes
    ref[B:, :] = as_codes(jnp.concatenate([exponent, rows], axis=0))


def load_scalars(ref):
    tail = ref[B:, :].astype(jnp.int32).astype(F32)
    return (tail[8:9, :] + tail[9:10, :] * (1.0 / 32768.0)) * jnp.exp2(tail[10:11, :] - 14.0)


def load_piece(ref):
    return decode(ref), load_scalars(ref)


def encode_kernel(at_ref, start_ref, codes_ref, half_ref, start, sem):
    copy = pltpu.make_async_copy(start_ref, start, sem)
    copy.start()
    copy.wait()
    half = fold_columns(start[0, half_rows(at_ref[0]), :])
    half_ref[...] = half
    rows = scalar_rows(jnp.broadcast_to(total_of(half * half), (8, LANES)))
    for s in range(SEC):
        store_piece(codes_ref.at[s], half, rows)


def decode_start(core, own_ref, other_ref, start_ref, x_ref, norm_ref, sums_ref):
    squares = load_scalars(own_ref.at[0]) + load_scalars(other_ref.at[0])
    for s in range(1, SEC):
        squares = squares + (load_scalars(own_ref.at[s]) + load_scalars(other_ref.at[s]))
    mean_sq = squares[:, :1] / ENTRIES
    scale = 1.0 / jnp.sqrt(mean_sq + 1e-06)
    norm_ref[0] = jnp.broadcast_to(scale, (8, LANES))
    norm_ref[1] = jnp.broadcast_to(mean_sq, (8, LANES))
    vec = start_ref[...] * scale
    wide = vec.astype(BF16).astype(F32)
    sums_ref[1] = fold(vec * wide) / CHIPS_X
    sums_ref[2] = fold(wide * wide) / CHIPS_X

    @pl.loop(0, SEC, unroll=2)
    def _(s):
        for ref, at in ((own_ref, core), (other_ref, 1 - core)):
            rounded = (decode(ref.at[s]) * scale).astype(BF16)
            x_ref[s, half_rows(at), :LANES] = rounded[:HALF, :]
            x_ref[s, half_rows(at), LANES:] = rounded[HALF:, :]


def head_kernel(left_ref, right_ref, left_out, right_out, sems):
    copies = [
        pltpu.make_async_copy(ref.at[pl.ds(0, STEP)], out, sems.at[k])
        for k, (ref, out) in enumerate(((left_ref, left_out), (right_ref, right_out)))
    ]
    for copy in copies:
        copy.start()
    for copy in copies:
        copy.wait()


def first_kernel(count_ref, from_ref, to_ref, at_ref, own_ref, other_ref, start_ref, left_head, right_head, left_ref, right_ref,
                 keep_ref, send_ref, sums_ref, norm_ref, left, right, x_ref, acc_ref, halves_ref, sems, term_sems):
    def prepare(core):
        decode_start(core, own_ref, other_ref, start_ref, x_ref, norm_ref, sums_ref)

    apply_terms(
        prepare, (count_ref, from_ref, to_ref, at_ref), (left_head, right_head), (left_ref, right_ref), (left, right),
        keep_ref, send_ref, sums_ref, x_ref, acc_ref, halves_ref, sems, term_sems,
    )


def second_kernel(count_ref, from_ref, to_ref, at_ref, own_ref, other_ref, more_ref, left_head, right_head,
                  left, right, keep_ref, send_ref, sums_ref, x_ref, acc_ref, halves_ref, sems):
    def prepare(core):
        copies = [
            pltpu.make_async_copy(own_ref, x_ref.at[:, half_rows(core), :], sems.at[0]),
            pltpu.make_async_copy(other_ref, x_ref.at[:, half_rows(1 - core), :], sems.at[1]),
        ]
        for copy in copies:
            copy.start()
        sums_ref[1:] = more_ref[...]
        for copy in copies:
            copy.wait()

    apply_terms(
        prepare, (count_ref, from_ref, to_ref, at_ref), (left_head, right_head), None, (left, right),
        keep_ref, send_ref, sums_ref, x_ref, acc_ref, halves_ref, sems, None,
    )


def apply_terms(prepare, terms, heads, far, held, keep_ref, send_ref, sums_ref, x_ref, acc_ref, halves_ref, sems,
                term_sems):
    count_ref, from_ref, to_ref, at_ref = terms
    core = at_ref[0]

    def term_copies(i):
        out = pl.ds(i * GROUP, GROUP)
        at = pl.ds(STEP + i * GROUP, GROUP)
        return [
            pltpu.make_async_copy(ref.at[at], to.at[out], term_sems.at[k, i])
            for k, (ref, to) in enumerate(zip(far, held))
        ]

    def fetch(i):
        @pl.when((i < GROUPS) & (STEP + i * GROUP < count_ref[0]))
        def _():
            for copy in term_copies(i):
                copy.start()

    if far:
        for i in range(AHEAD):
            fetch(i)

    @pl.loop(0, SEC)
    def _(s):
        acc_ref[s] = jnp.zeros((B, B), F32)

    prepare(core)

    def step(i, lefts, rights, base):
        live = count_ref[0] - i * STEP

        def first_half(j):
            t = i * STEP + j
            block = lefts[base + j]
            halves_ref[2 * j] = dot(block, x_ref[from_ref[t]], (1, 0)).astype(BF16)
            halves_ref[2 * j + 1] = dot(block, x_ref[to_ref[t]], (0, 0)).astype(BF16)

        def second_half(j):
            t = i * STEP + j
            block = rights[base + j]
            acc_ref[to_ref[t]] += dot(halves_ref[2 * j], block, (1, 1))
            acc_ref[from_ref[t]] += dot(halves_ref[2 * j + 1], block, (1, 0))

        @pl.when(live >= STEP)
        def _():
            for j in range(STEP):
                first_half(j)
            for j in range(STEP):
                second_half(j)

        @pl.when((live > 0) & (live < STEP))
        def _():
            @pl.loop(0, live)
            def _(j):
                first_half(j)
                second_half(j)

    step(0, *heads, 0)

    @pl.loop(0, TERMS // STEP - 1)
    def _(i):
        for k in range(STEP // GROUP if far else 0):
            @pl.when(count_ref[0] > (i + 1) * STEP + k * GROUP)
            def _():
                for copy in term_copies(i * (STEP // GROUP) + k):
                    copy.wait()

            fetch(i * (STEP // GROUP) + k + AHEAD)

        step(i + 1, *held, i * STEP)

    keep_copy = pltpu.make_async_copy(acc_ref.at[:, half_rows(core), :], keep_ref, sems.at[0])
    keep_copy.start()

    def inner(s, total):
        mine, theirs = half_rows(core), half_rows(1 - core)
        part = acc_ref[s, theirs, :]
        send_ref[s] = part.astype(BF16)
        total = total + fold(x_ref[s, theirs, :].astype(F32) * part)
        return total + fold(x_ref[s, mine, :].astype(F32) * acc_ref[s, mine, :])

    sums_ref[0] = lax.fori_loop(0, SEC, inner, jnp.zeros((8, LANES), F32))
    keep_copy.wait()


def join_kernel(keep_ref, got_ref, sums_ref, got_sums_ref, out_ref):
    lane = lax.broadcasted_iota(jnp.int32, (8, LANES), 1)
    scalars = jnp.zeros((8, LANES), F32)
    for k in range(sums_ref.shape[0]):
        scalars = jnp.where(lane == k, total_of(sums_ref[k] + got_sums_ref[k]), scalars)
    rows = scalar_rows(scalars)

    @pl.loop(0, SEC, unroll=4)
    def _(s):
        store_piece(out_ref.at[s], fold_columns(keep_ref[s] + got_ref[s].astype(F32)), rows)


def sum_kernel(got_ref, out_ref):
    def add(s, totals):
        half, scalars = load_piece(got_ref.at[s])
        return totals[0] + half, totals[1] + scalars

    zeros = jnp.zeros((B, LANES), F32), jnp.zeros((1, LANES), F32)
    half, scalars = lax.fori_loop(0, SEC, add, zeros, unroll=4)
    store_piece(out_ref, half, scalar_rows(jnp.broadcast_to(scalars, (8, LANES))))


def sum_of_chips(part_refs, count):
    own, near, across, far = (load_piece(ref) for ref in part_refs)
    half, scalars = ((own[k] + across[k]) + (near[k] + far[k]) for k in range(2))
    lane = lax.broadcasted_iota(jnp.int32, scalars.shape, 1)
    return half, [total_of(jnp.where(lane == k, scalars, 0.0)) / ENTRIES for k in range(count)]


def correct_kernel(at_ref, own_ref, near_ref, across_ref, far_ref, start_ref, diag_ref, norm_ref, copies_ref, sums_ref, corr_ref, sigma_ref, theta_ref):
    sigma, (theta, vec_round, round_sq) = sum_of_chips((own_ref, near_ref, across_ref, far_ref), 3)
    theta = theta * ratio(vec_round, round_sq)
    vec = start_ref[...] * norm_ref[0, :1, :1]
    diag = fold_columns(diag_ref[0, half_rows(at_ref[0]), :])
    corr = (sigma - theta * vec) / jnp.maximum(jnp.abs(diag - theta), 1.0)
    sigma_ref[...] = sigma
    corr_ref[...] = corr
    theta_ref[...] = jnp.broadcast_to(theta, theta_ref.shape)
    rounded = corr.astype(BF16)
    for s in range(SEC):
        store_half(copies_ref, s, rounded)
    wide = rounded.astype(F32)
    pairs = ((vec, corr), (corr, corr), (sigma, corr), (corr, wide), (wide, wide))
    for k, (one, two) in enumerate(pairs):
        sums_ref[k] = fold(one * two) / CHIPS_X


def ritz_kernel(own_ref, near_ref, across_ref, far_ref, start_ref, norm_ref, corr_ref, sigma_ref, theta_ref, out_ref):
    h_corr, (quad, along, corr_sq, cross, corr_round, round_sq) = sum_of_chips((own_ref, near_ref, across_ref, far_ref), 6)
    theta, scale, mean_sq = theta_ref[:1, :1], norm_ref[0, :1, :1], norm_ref[1, :1, :1]
    quad = quad * ratio(corr_round, round_sq)
    vec_sq = mean_sq * scale * scale
    ortho_sq = jnp.maximum(corr_sq - along * along * (2.0 - vec_sq), 0.0)
    inv = 1.0 / jnp.sqrt(ortho_sq + 1e-06)
    beta = (cross - along * theta) * inv
    gamma = (quad - 2.0 * along * cross + along * along * theta) * inv * inv
    lowest = 0.5 * (theta + gamma) - jnp.sqrt((0.5 * (theta - gamma)) ** 2 + beta * beta)
    norm = jnp.sqrt(beta * beta + (lowest - theta) ** 2)
    one, two = beta / norm, (lowest - theta) / norm
    vec, sigma = start_ref[...] * scale, sigma_ref[...]
    vec_two, sigma_two = (corr_ref[...] - along * vec) * inv, (h_corr - along * sigma) * inv
    ritz = one * vec + two * vec_two
    store_half(out_ref, 0, ritz)
    store_half(out_ref, 1, one * sigma + two * sigma_two - lowest * ritz)


def place_kernel(at_ref, own_ref, other_ref, vector_ref, residual_ref):
    core = at_ref[0]
    for k, ref in enumerate((vector_ref, residual_ref)):
        ref[0, half_rows(core), :] = own_ref[k]
        ref[0, half_rows(1 - core), :] = other_ref[k]


def shape(*dims, dtype=F32):
    return jax.ShapeDtypeStruct(dims, dtype)


SMEM = pl.BlockSpec(memory_space=pltpu.SMEM)
WHOLE = pl.BlockSpec(memory_space=pltpu.VMEM)
ANY = pl.BlockSpec(memory_space=pl.ANY)
GATHER = shape(SEC, HALF, B, dtype=BF16)
COLUMNS = shape(B, LANES)
PIECES = shape(SEC, B + 16, LANES, dtype=jnp.int16)


def call(kernel, mib, ins, outs, *args, **kwargs):
    return pl.pallas_call(
        kernel,
        out_shape=outs,
        in_specs=ins,
        compiler_params=pltpu.CompilerParams(vmem_limit_bytes=mib << 20),
        name=kernel.__name__,
        **kwargs,
    )(*args)


def swap(x):
    return lax.ppermute(x, "op", CORE_SWAP)


def over_sectors(x):
    return lax.all_to_all(x, "sec", 0, 0, tiled=True)


def in_hbm(*arrays):
    return [pltpu.with_memory_space_constraint(x, pltpu.HBM) for x in arrays]


def terms_shape(count):
    return [shape(count, B, B, dtype=BF16)] * 2


APPLY_SCRATCH = [
    pltpu.VMEM((SEC, B, B), BF16),
    pltpu.VMEM((SEC, B, B), F32),
    pltpu.VMEM((2 * STEP, B, B), BF16),
    pltpu.SemaphoreType.DMA((2,)),
]
SPLIT = [shape(SEC, HALF, B), GATHER]


def reduce_partial(keep, send, sums):
    payload = call(
        join_kernel, 16, [WHOLE] * 4, PIECES,
        keep, swap(send), sums, swap(sums),
    )
    part = call(sum_kernel, 16, [WHOLE], shape(B + 16, LANES, dtype=jnp.int16), over_sectors(payload))
    return part, *(lax.ppermute(part, "op", perm) for perm in ALONG_X)


def per_device(start_vector, diag_guess, left_env, right_env, sector_from, sector_to, term_count):
    at = (lax.axis_index("op") % 2).astype(jnp.int32).reshape(1)
    terms = (term_count, sector_from, sector_to, at)
    codes, start = call(
        encode_kernel, 16, [SMEM, ANY], [PIECES, COLUMNS],
        at, *in_hbm(start_vector),
        scratch_shapes=[pltpu.VMEM((1, B, B), F32), pltpu.SemaphoreType.DMA],
    )
    far = in_hbm(left_env, right_env)
    head = call(
        head_kernel, 16, [ANY] * 2, terms_shape(STEP), *far,
        out_specs=[WHOLE] * 2, scratch_shapes=[pltpu.SemaphoreType.DMA((2,))],
    )
    own = over_sectors(codes)
    keep, send, sums, norm, *held = call(
        first_kernel, 28, [SMEM] * 4 + [WHOLE] * 5 + [ANY] * 2,
        SPLIT + [shape(3, 8, LANES), shape(2, 8, LANES)] + terms_shape(TERMS - STEP),
        *terms, own, swap(own), start, *head, *far,
        out_specs=[ANY] + [WHOLE] * 5,
        scratch_shapes=APPLY_SCRATCH + [pltpu.SemaphoreType.DMA((2, GROUPS))],
    )
    got = reduce_partial(keep, send, sums)
    copies, more, corr, sigma, theta = call(
        correct_kernel, 16, [SMEM] + [WHOLE] * 7,
        [GATHER, shape(5, 8, LANES), COLUMNS, COLUMNS, shape(8, LANES)],
        at, *got, start, diag_guess, norm,
    )
    own = over_sectors(copies)
    keep, send, sums = call(
        second_kernel, 28, [SMEM] * 4 + [ANY] * 2 + [WHOLE] * 5,
        SPLIT + [shape(6, 8, LANES)],
        *terms, own, swap(own), more, *head, *held,
        out_specs=[ANY] + [WHOLE] * 2,
        scratch_shapes=APPLY_SCRATCH,
    )
    got = reduce_partial(keep, send, sums)
    halves = call(ritz_kernel, 16, [WHOLE] * 9, shape(2, HALF, B), *got, start, norm, corr, sigma, theta)
    return call(
        place_kernel, 16, [SMEM] + [WHOLE] * 2, [shape(1, B, B), shape(1, B, B)], at, halves, swap(halves)
    )


def solution(mesh):
    return jax.shard_map(
        per_device,
        mesh=mesh,
        in_specs=(
            P("sec", None, None),
            P("sec", None, None),
            P(("op", "sec"), None, None),
            P(("op", "sec"), None, None),
            P(("op", "sec")),
            P(("op", "sec")),
            P(("op", "sec")),
        ),
        out_specs=(P("sec", None, None), P("sec", None, None)),
        check_vma=False,
    )
```
